512 devices in a mesh: gx: 32 (over z, x_lo, core), gy: 16 (over x_hi, y).
Axes of the slice: x: 4 (x_hi: 2, x_lo: 2; x = x_hi * 2 + x_lo), y: 8, z: 8, core: 2. Of those that a mesh axis runs over, the one named last changes fastest.
Arguments:
- feat_in: bfloat16 [64, 192, 32, 128], P('gx', 'gy'), may hold values from -6 to 6
- conv_out: bfloat16 [64, 192, 32, 128], P('gx', 'gy'), may hold values from -30 to 30
- activ: bfloat16 [64, 192, 32, 128], P('gx', 'gy'), may hold values from -6 to 6
- weight: bfloat16 [3456, 128], replicated, may hold values from -0.109375 to 0.109375
- gain: float32 [128], replicated, may hold values from 0.1 to 1.9
- head: float32 [3, 128], replicated, may hold values from -3 to 3
- labels: int32 [64, 192, 32], P('gx', 'gy'), may hold values from 0 to 2
- grad_up: bfloat16 [64, 192, 32, 128], P('gx', 'gy'), may hold values from -8 to 8
Outputs:
- grad_in: bfloat16 [64, 192, 32, 128], P('gx', 'gy')
- grad_weight: bfloat16 [3456, 128], replicated
- gain_gradient: float32 [128], replicated
- shift_gradient: float32 [128], replicated
The draws below stay inside these ranges and needn't reach their ends.
All inputs are finite; a program needn't handle non-finite values.
Results may differ from the reference program's by a relative error of at most 0.02.
Values may be sent and summed in bfloat16 or wider, within the bound.
A program may use at most 64 MiB of HBM per device.

```python
import jax
import jax.numpy as jnp
from jax import lax

C = 128
K = 3
NX = 64
NY = 192
NZ = 32


def shared_base(key):
    return jax.random.normal(key, (NX, NY, NZ, C), jnp.float32)


def draw_conv_out(key, part):
    raw = shared_base(key)
    key = jax.random.fold_in(key, 11)
    key_chan, key_off, key_tilt = jax.random.split(key, 3)
    chan = jnp.exp(jax.random.uniform(key_chan, (C,), jnp.float32, -0.5, 0.5))
    offset = jnp.clip(0.3 * jax.random.normal(key_off, (C,), jnp.float32), -1.2, 1.2)
    tilt = jax.random.uniform(key_tilt, (C,), jnp.float32, -0.5, 0.5)
    along_x = (jnp.arange(NX, dtype=jnp.float32) / NX)[:, None, None, None]
    along_y = (jnp.arange(NY, dtype=jnp.float32) / NY)[None, :, None, None]
    base = jnp.clip(raw, -4.5, 4.5)
    ramp = (0.6 + 0.8 * along_x) * (0.5 + 1.5 * along_y)
    level = offset + 2.0 * tilt * (along_y - 0.5)
    return ((level + base) * chan * ramp).astype(jnp.bfloat16)


def draw_grad_up(key, part):
    raw = shared_base(key)
    key = jax.random.fold_in(key, 23)
    key_off, key_rho, key_noise = jax.random.split(key, 3)
    rho = jax.random.uniform(key_rho, (C,), jnp.float32, 0.3, 0.8)
    noise = jax.random.normal(key_noise, (NX, NY, NZ, C), jnp.float32)
    base = jnp.clip(raw, -4.5, 4.5)
    offset = 0.5 * jnp.clip(jax.random.normal(key_off, (C,), jnp.float32), -3.0, 3.0)
    return jnp.clip(offset + rho * base + noise, -8.0, 8.0).astype(jnp.bfloat16)


def set_ends(entries, own_key, least, high):
    longest = entries.shape.index(max(entries.shape))
    spots = []
    for shift in (0, 1):
        where = [jax.random.randint(jax.random.fold_in(own_key, axis), (), 0, length) for axis, length in enumerate(entries.shape)]
        where[longest] = (where[longest] + shift) % entries.shape[longest]
        spots.append(tuple(where))
    return entries.at[spots[0]].set(least).at[spots[1]].set(high)


def shard_levels(key, dims, cuts, low, high):
    level, own = 1.0, jax.random.fold_in(key, 6)
    for position, parts in cuts:
        draws = jnp.exp(jax.random.uniform(jax.random.fold_in(own, position), (parts,), jnp.float32, low / len(cuts), high / len(cuts)))
        level = level * jnp.repeat(draws, dims[position] // parts).reshape([-1 if axis == position else 1 for axis in range(len(dims))])
    return level


def bell_draw(key, dims, width, reach, cuts=(), kind=jnp.bfloat16):
    entries = width * jax.random.normal(key, dims, jnp.float32)
    if cuts:
        entries = entries * shard_levels(key, dims, cuts, -0.22, 0.18)
    return jnp.clip(entries, -reach, reach).astype(kind)


def setup_inputs(seed: int = 0) -> dict:
    key_of = jax.random.split(jax.random.key(seed), 9)
    feat_in = bell_draw(key_of[0], (NX, NY, NZ, C), 1.0, 6.0, ((0, 32), (1, 16)))
    conv_out = draw_conv_out(jax.random.fold_in(key_of[8], 71), 0)
    activ = bell_draw(key_of[2], (NX, NY, NZ, C), 1.0, 6.0, ((0, 32), (1, 16)))
    weight = bell_draw(key_of[3], (27 * C, C), (27 * C) ** -0.5, 0.109375)
    gain = jnp.clip(1.0 + 0.18 * jax.random.normal(key_of[4], (C,), jnp.float32), 0.1, 1.9)
    head = bell_draw(key_of[5], (K, C), 0.5, 3.0, (), jnp.float32)
    labels = set_ends(jax.random.randint(key_of[6], (NX, NY, NZ), 0, K), jax.random.fold_in(key_of[6], 1), 0, K - 1).astype(jnp.int32)
    grad_up = draw_grad_up(jax.random.fold_in(key_of[8], 71), 0)
    return {"feat_in": feat_in, "conv_out": conv_out, "activ": activ, "weight": weight, "gain": gain, "head": head, "labels": labels, "grad_up": grad_up}


def reference(feat_in, conv_out, activ, weight, gain, head, labels, grad_up):
    voxel_total = NX * NY * NZ * 1.0
    hidden_complete = conv_out.astype(jnp.float32)
    channel_mean = lax.optimization_barrier(jnp.sum(hidden_complete, axis=(0, 1, 2))) / voxel_total
    meansq = lax.optimization_barrier(jnp.sum(hidden_complete * hidden_complete, axis=(0, 1, 2))) / voxel_total
    inverse_deviation = lax.rsqrt(meansq - channel_mean * channel_mean + 1e-05)
    normalized_input = (hidden_complete - channel_mean) * inverse_deviation
    act = activ.astype(jnp.float32)
    logits = jnp.einsum('xyzc,kc->xyzk', act, head, precision=lax.Precision.HIGHEST)
    onehot = (labels[..., None] == jnp.arange(K, dtype=jnp.int32)).astype(jnp.float32)
    dz = 0.5 * (jax.nn.sigmoid(logits) - onehot)
    ga = grad_up.astype(jnp.float32) + jnp.einsum('xyzk,kc->xyzc', dz, head, precision=lax.Precision.HIGHEST)
    normed_gradient = jnp.where(act > 0, ga, 0.01 * ga)
    shift_gradient = lax.optimization_barrier(jnp.sum(normed_gradient, axis=(0, 1, 2)))
    gain_gradient = lax.optimization_barrier(jnp.sum(normed_gradient * normalized_input, axis=(0, 1, 2)))
    hidden_gradient = (gain * inverse_deviation * (normed_gradient - shift_gradient / voxel_total - normalized_input * gain_gradient / voxel_total)).astype(jnp.bfloat16)
    dpad = jnp.pad(hidden_gradient, ((1, 1), (1, 1), (1, 1), (0, 0)))
    flat_in = feat_in.reshape(-1, C)
    total = jnp.zeros((NX * NY * NZ, C), jnp.float32)
    blocks = []
    for step_a in (-1, 0, 1):
        for step_b in (-1, 0, 1):
            for step_c in (-1, 0, 1):
                tap = (step_a + 1) * 9 + (step_b + 1) * 3 + (step_c + 1)
                moved = dpad[1 - step_a:1 - step_a + NX, 1 - step_b:1 - step_b + NY, 1 - step_c:1 - step_c + NZ].reshape(-1, C)
                wtap = weight[tap * C:(tap + 1) * C]
                total = total + jnp.dot(moved, wtap.T, preferred_element_type=jnp.float32)
                blocks.append(jnp.dot(flat_in.T, moved, preferred_element_type=jnp.float32))
    grad_in = total.reshape(NX, NY, NZ, C).astype(jnp.bfloat16)
    grad_weight = jnp.concatenate(blocks, axis=0).astype(jnp.bfloat16)
    return (grad_in, grad_weight, gain_gradient, shift_gradient)
```

```python
import functools

import jax
import jax.numpy as jnp
from jax import lax
from jax.experimental import pallas as pl
from jax.experimental.pallas import tpu as pltpu
from jax.sharding import PartitionSpec as P

MESH = pl.DeviceIdType.MESH
F32 = jnp.float32
BF16 = jnp.bfloat16
C = 128
X, Y, Z = 2, 12, 32
COLS = X * Y
VOX = COLS * Z
PLANE = Y * Z
HALF = 14 * C
CORE_T = BF16
YP, ZP, XP = 64, 64, 192
YO, ZO, XO = 0, 8 * YP, 8 * YP + 8 * ZP


def ring(n):
    order = sorted(range(1, n), key=lambda k: -min(k, n - k))
    return order


def kernel(
    total_voxels,
    feat, conv, activ, weight, gain, head, labels, grad_up,
    gin_out, gw_out, gg_out, sg_out,
    fpad, dpad, conv_v, act_v, gu_v, w_v, lab_s, dn_s, dhc_s, ft_s, g_s, gin_v,
    rc, rx, ry, rz,
    core_in, h_s,
    y1, z1, x1, y2, z2, x2, y3, z3, x3, y4, z4, x4, s2y, s2z, s2x, gwbuf,
    lsem, ssem, rsem, hsem, hrsem,
):
    gx, gy = lax.axis_index("gx"), lax.axis_index("gy")
    z, xl, c = gx // 4, (gx // 2) % 2, gx % 2
    xh, y = gy // 8, gy % 8
    x = xh * 2 + xl

    def at_core():
        return (z * 4 + xl * 2 + (1 - c), gy)

    def at_x(j):
        return (z * 4 + (j % 2) * 2 + c, (j // 2) * 8 + y)

    def at_y(j):
        return (gx, xh * 8 + j)

    def at_z(j):
        return (j * 4 + xl * 2 + c, gy)

    up_x, down_x = (gx + 1) % 32, (gx + 31) % 32
    up_y, down_y = (gy + 1) % 16, (gy + 15) % 16

    barrier = pltpu.get_barrier_semaphore()
    partners = [at_core()]
    partners += [at_x((x + k) % 4) for k in ring(4)]
    partners += [at_y((y + k) % 8) for k in ring(8)]
    partners += [at_z((z + k) % 8) for k in ring(8)]
    partners += [(i, j) for i in (down_x, gx, up_x) for j in (down_y, gy, up_y)
                 if not (i is gx and j is gy)]
    for p in partners:
        pl.semaphore_signal(barrier, inc=1, device_id=p, device_id_type=MESH)

    loads = [
        pltpu.make_async_copy(activ, act_v, lsem.at[0]),
        pltpu.make_async_copy(conv, conv_v, lsem.at[1]),
        pltpu.make_async_copy(grad_up, gu_v, lsem.at[2]),
        pltpu.make_async_copy(feat, fpad.at[pl.ds(1, X), pl.ds(1, Y)], lsem.at[3]),
        pltpu.make_async_copy(weight, w_v, lsem.at[4]),
    ]
    for cp in loads:
        cp.start()

    pending = []

    def send(src, dst, sems, rsems, i, dev):
        cp = pltpu.make_async_remote_copy(
            src_ref=src, dst_ref=dst, send_sem=sems.at[i], recv_sem=rsems.at[i],
            device_id=dev, device_id_type=MESH,
        )
        cp.start()
        return cp

    def ring_exchange(stage, n, me, where, src, dst, count):
        for k in ring(n):
            j = (me + k) % n
            send(src(j), dst(me), ssem, rsem, stage, where(j))
        pending.append((stage, count))

    def wait_bytes(sem, ref):
        pltpu.make_async_copy(ref, ref, sem).wait()

    def rim(buf, base):
        inner_x, inner_y = pl.ds(1, X), pl.ds(1, Y)
        moves = [
            (pl.ds(X, 1), inner_y, pl.ds(0, 1), inner_y, (up_x, gy)),
            (pl.ds(1, 1), inner_y, pl.ds(X + 1, 1), inner_y, (down_x, gy)),
            (inner_x, pl.ds(Y, 1), inner_x, pl.ds(0, 1), (gx, up_y)),
            (inner_x, pl.ds(1, 1), inner_x, pl.ds(Y + 1, 1), (gx, down_y)),
            (pl.ds(X, 1), pl.ds(Y, 1), pl.ds(0, 1), pl.ds(0, 1), (up_x, up_y)),
            (pl.ds(X, 1), pl.ds(1, 1), pl.ds(0, 1), pl.ds(Y + 1, 1), (up_x, down_y)),
            (pl.ds(1, 1), pl.ds(Y, 1), pl.ds(X + 1, 1), pl.ds(0, 1), (down_x, up_y)),
            (pl.ds(1, 1), pl.ds(1, 1), pl.ds(X + 1, 1), pl.ds(Y + 1, 1), (down_x, down_y)),
        ]
        return [
            send(buf.at[sx, sy], buf.at[dx, dy], hsem, hrsem, base + i, dev)
            for i, (sx, sy, dx, dy, dev) in enumerate(moves)
        ]

    def clear_rim(buf):
        @pl.when(gx == 0)
        def _():
            buf[0:1] = jnp.zeros((1, Y + 2, Z, C), BF16)

        @pl.when(gx == 31)
        def _():
            buf[X + 1 : X + 2] = jnp.zeros((1, Y + 2, Z, C), BF16)

        @pl.when(gy == 0)
        def _():
            buf[:, 0:1] = jnp.zeros((X + 2, 1, Z, C), BF16)

        @pl.when(gy == 15)
        def _():
            buf[:, Y + 1 : Y + 2] = jnp.zeros((X + 2, 1, Z, C), BF16)

    lab_s[...] = jnp.zeros_like(lab_s)
    for i in range(X):
        lab_s[pl.ds(16 * i, Y), pl.ds(0, Z)] = labels[i].astype(F32)
    lab_t = jnp.transpose(lab_s[...])[0:Z]

    row = lax.broadcasted_iota(jnp.int32, (C, C), 0)
    rep = jnp.zeros((C, C), F32)
    for k in range(3):
        rep = jnp.where(row % 3 == k, head[k : k + 1, :], rep)
    rep = jnp.where(row < 18, rep, 0.0)
    hi = rep.astype(BF16)
    left = rep - hi.astype(F32)
    mid = left.astype(BF16)
    low = (left - mid.astype(F32)).astype(BF16)
    part = row // 3
    back = jnp.where(
        (part == 0) | (part == 3) | (part == 5), hi.astype(F32),
        jnp.where((part == 1) | (part == 4), mid.astype(F32),
                  jnp.where(part == 2, low.astype(F32), 0.0)),
    ).astype(BF16)
    lane = lax.broadcasted_iota(jnp.int32, (C, C), 1)
    lane_class = (lane % 3).astype(F32)

    NT = (((1,), (1,)), ((), ()))

    loads[0].wait()
    loads[1].wait()
    loads[2].wait()
    sums = [jnp.zeros((8, C), F32) for _ in range(4)]
    step = C
    for t in range(VOX // step):
        xi, yi = (4 * t) // Y, (4 * t) % Y
        act = act_v[xi, yi : yi + 4].reshape(step, C)
        logits = (
            lax.dot_general(act, hi, NT, preferred_element_type=F32)
            + lax.dot_general(act, mid, NT, preferred_element_type=F32)
            + lax.dot_general(act, low, NT, preferred_element_type=F32)
        )
        label = jnp.concatenate(
            [jnp.broadcast_to(lab_t[:, 16 * xi + yi + q : 16 * xi + yi + q + 1], (Z, C)) for q in range(4)],
            axis=0,
        )
        dz = 0.5 * (jax.nn.sigmoid(logits) - (label == lane_class).astype(F32))
        dz_hi = dz.astype(BF16).astype(F32)
        dz_left = dz - dz_hi
        dz_mid = dz_left.astype(BF16).astype(F32)
        dz_low = dz_left - dz_mid
        spread = jnp.where(lane < 9, dz_hi, jnp.where(lane < 15, dz_mid, dz_low)).astype(BF16)
        ga = gu_v[xi, yi : yi + 4].reshape(step, C).astype(F32) + jnp.dot(
            spread, back, preferred_element_type=F32
        )
        dn = jnp.where(act.astype(F32) > 0, ga, 0.01 * ga)
        dn_s[pl.ds(t * step, step)] = dn
        h = conv_v[xi, yi : yi + 4].reshape(step, C).astype(F32)
        for i, term in enumerate((h, h * h, dn, dn * h)):
            sums[i] = sums[i] + jnp.sum(term.reshape(step // 8, 8, C), axis=0)
    stats = jnp.concatenate(
        [jnp.sum(s, axis=0, keepdims=True) for s in sums] + [jnp.zeros((4, C), F32)], axis=0
    )

    pl.semaphore_wait(barrier, len(partners))

    rc[c] = stats
    send(rc.at[c], rc.at[c], ssem, rsem, 0, at_core())
    pending.append((0, rc.at[pl.ds(0, 1)]))
    loads[3].wait()
    feat_rim = rim(fpad, 0)
    wait_bytes(rsem.at[0], rc.at[pl.ds(0, 1)])
    stats = rc[0] + rc[1]
    for stage, n, me, where, buf in ((1, 4, x, at_x, rx), (2, 8, y, at_y, ry), (3, 8, z, at_z, rz)):
        buf[me] = stats
        ring_exchange(stage, n, me, where, lambda j: buf.at[me], lambda j: buf.at[j], buf.at[pl.ds(0, n - 1)])
        if stage == 3:
            for cp in feat_rim:
                cp.wait_recv()
            clear_rim(fpad)
            for pln in range(X + 2):
                for b in range(3):
                    block = fpad[pln, b : b + Y].reshape(PLANE, C)
                    ft_s[pl.ds((pln * 3 + b) * C, C)] = jnp.transpose(block)
            loads[4].wait()
        wait_bytes(rsem.at[stage], buf.at[pl.ds(0, n - 1)])
        stats = buf[0]
        for j in range(1, n):
            stats = stats + buf[j]

    mean = stats[0:1] / total_voxels
    rstd = lax.rsqrt(stats[1:2] / total_voxels - mean * mean + 1e-05)
    shift_grad = stats[2:3]
    gain_grad = rstd * (stats[3:4] - mean * shift_grad)
    gg_out[...] = gain_grad
    sg_out[...] = shift_grad
    scale = gain[...] * rstd
    shift_mean = shift_grad / total_voxels
    gain_mean = gain_grad / total_voxels

    zrow = lax.broadcasted_iota(jnp.int32, (step, C), 0) % Z
    for t in range(VOX // step):
        xi, yi = (4 * t) // Y, (4 * t) % Y
        h = conv_v[xi, yi : yi + 4].reshape(step, C).astype(F32)
        dh = scale * (dn_s[pl.ds(t * step, step)] - shift_mean - (h - mean) * rstd * gain_mean)
        mid_dh = dh.astype(BF16)
        dpad[1 + xi, 1 + yi : 5 + yi] = mid_dh.reshape(4, Z, C)
        after = jnp.where(zrow == Z - 1, 0.0, pltpu.roll(dh, step - 1, 0))
        before = jnp.where(zrow == 0, 0.0, pltpu.roll(dh, 1, 0))
        rows = pl.ds(t * step, step)
        dhc_s[rows, 0:C] = after.astype(BF16)
        dhc_s[rows, C : 2 * C] = mid_dh
        dhc_s[rows, 2 * C : 3 * C] = before.astype(BF16)
    dh_rim = rim(dpad, 8)

    for ab in range(9):
        block = jnp.dot(
            ft_s[pl.ds(ab * C, C)], dhc_s[0:PLANE], preferred_element_type=F32
        ) + jnp.dot(
            ft_s[pl.ds((ab + 3) * C, C)], dhc_s[PLANE : 2 * PLANE], preferred_element_type=F32
        )
        for k in range(3):
            g_s[pl.ds((ab * 3 + k) * C, C)] = block[:, k * C : (k + 1) * C].astype(CORE_T)
    g_s[pl.ds(27 * C, C)] = jnp.zeros((C, C), CORE_T)

    mine = pl.multiple_of(c * HALF, HALF)
    others = pl.multiple_of((1 - c) * HALF, HALF)
    send(g_s.at[pl.ds(others, HALF)], core_in, ssem, rsem, 4, at_core())
    pending.append((4, core_in))
    wait_bytes(rsem.at[4], core_in)
    for t in range(14):
        rows = pl.ds(t * C, C)
        h_s[rows] = (
            g_s[pl.ds(pl.multiple_of(mine + t * C, C), C)].astype(F32) + core_in[rows].astype(F32)
        ).astype(BF16)

    def chunk(base, size):
        return lambda j: h_s.at[pl.ds(pl.multiple_of(base + j * size, 64), size)]

    ring_exchange(5, 8, y, at_y, chunk(YO, YP), lambda j: y1.at[j], y1.at[pl.ds(0, 7)])
    ring_exchange(6, 8, z, at_z, chunk(ZO, ZP), lambda j: z1.at[j], z1.at[pl.ds(0, 7)])
    ring_exchange(7, 4, x, at_x, chunk(XO, XP), lambda j: x1.at[j], x1.at[pl.ds(0, 3)])
    y1[y] = h_s[pl.ds(pl.multiple_of(YO + y * YP, YP), YP)]
    z1[z] = h_s[pl.ds(pl.multiple_of(ZO + z * ZP, ZP), ZP)]
    x1[x] = h_s[pl.ds(pl.multiple_of(XO + x * XP, 64), XP)]

    for cp in dh_rim:
        cp.wait_recv()
    clear_rim(dpad)
    for i in range(X):
        total = jnp.zeros((PLANE, 3 * C), F32)
        for ab in range(9):
            a, b = ab // 3, ab % 3
            moved = dpad[i + 2 - a, 2 - b : 2 - b + Y].reshape(PLANE, C)
            total = total + lax.dot_general(
                moved, w_v[pl.ds(ab * 3 * C, 3 * C)], NT, preferred_element_type=F32
            )
        zr = lax.broadcasted_iota(jnp.int32, (PLANE, C), 0) % Z
        minus = jnp.where(zr == Z - 1, 0.0, pltpu.roll(total[:, 0:C], PLANE - 1, 0))
        plus = jnp.where(zr == 0, 0.0, pltpu.roll(total[:, 2 * C : 3 * C], 1, 0))
        gin_v[i] = (total[:, C : 2 * C] + minus + plus).astype(BF16).reshape(Y, Z, C)
    gin_copy = pltpu.make_async_copy(gin_v, gin_out, lsem.at[5])
    gin_copy.start()

    def add_up(buf, n):
        acc = buf[0].astype(F32)
        for j in range(1, n):
            acc = acc + buf[j].astype(F32)
        return acc

    wait_bytes(rsem.at[5], y1.at[pl.ds(0, 7)])
    s2y[...] = add_up(y1, 8).reshape(8, YP // 8, C)
    y2[z] = s2y[z]
    ring_exchange(8, 8, z, at_z, lambda j: s2y.at[j], lambda j: y2.at[j], y2.at[pl.ds(0, 7)])
    wait_bytes(rsem.at[6], z1.at[pl.ds(0, 7)])
    s2z[...] = add_up(z1, 8).reshape(8, ZP // 8, C)
    z2[y] = s2z[y]
    ring_exchange(9, 8, y, at_y, lambda j: s2z.at[j], lambda j: z2.at[j], z2.at[pl.ds(0, 7)])
    wait_bytes(rsem.at[7], x1.at[pl.ds(0, 3)])
    s2x[...] = add_up(x1, 4).reshape(8, XP // 8, C)
    x2[y] = s2x[y]
    ring_exchange(10, 8, y, at_y, lambda j: s2x.at[j], lambda j: x2.at[j], x2.at[pl.ds(0, 7)])

    wait_bytes(rsem.at[10], x2.at[pl.ds(0, 7)])
    x3[z] = add_up(x2, 8)
    ring_exchange(11, 8, z, at_z, lambda j: x3.at[z], lambda j: x3.at[j], x3.at[pl.ds(0, 7)])
    wait_bytes(rsem.at[8], y2.at[pl.ds(0, 7)])
    y3[x] = add_up(y2, 8)
    ring_exchange(12, 4, x, at_x, lambda j: y3.at[x], lambda j: y3.at[j], y3.at[pl.ds(0, 3)])
    wait_bytes(rsem.at[9], z2.at[pl.ds(0, 7)])
    z3[x] = add_up(z2, 8)
    ring_exchange(13, 4, x, at_x, lambda j: z3.at[x], lambda j: z3.at[j], z3.at[pl.ds(0, 3)])

    wait_bytes(rsem.at[12], y3.at[pl.ds(0, 3)])
    y4[z] = add_up(y3, 4)
    ring_exchange(14, 8, z, at_z, lambda j: y4.at[z], lambda j: y4.at[j], y4.at[pl.ds(0, 7)])
    wait_bytes(rsem.at[13], z3.at[pl.ds(0, 3)])
    z4[y] = add_up(z3, 4)
    ring_exchange(15, 8, y, at_y, lambda j: z4.at[y], lambda j: z4.at[j], z4.at[pl.ds(0, 7)])
    wait_bytes(rsem.at[11], x3.at[pl.ds(0, 7)])
    x4[y] = add_up(x3, 8)
    ring_exchange(16, 8, y, at_y, lambda j: x4.at[y], lambda j: x4.at[j], x4.at[pl.ds(0, 7)])

    def place(base, size):
        return lambda j: gwbuf.at[pl.ds(pl.multiple_of(mine + base + j * size, 64), size)]

    wait_bytes(rsem.at[14], y4.at[pl.ds(0, 7)])
    place_y = place(YO, YP)
    place_y(y)[...] = y4[...].reshape(YP, C).astype(BF16)
    ring_exchange(17, 8, y, at_y, lambda j: place_y(y), place_y, gwbuf.at[pl.ds(0, 7 * YP)])
    wait_bytes(rsem.at[15], z4.at[pl.ds(0, 7)])
    place_z = place(ZO, ZP)
    place_z(z)[...] = z4[...].reshape(ZP, C).astype(BF16)
    ring_exchange(18, 8, z, at_z, lambda j: place_z(z), place_z, gwbuf.at[pl.ds(0, 7 * ZP)])
    wait_bytes(rsem.at[16], x4.at[pl.ds(0, 7)])
    place_x = place(XO, XP)
    place_x(x)[...] = x4[...].reshape(XP, C).astype(BF16)
    ring_exchange(19, 4, x, at_x, lambda j: place_x(x), place_x, gwbuf.at[pl.ds(0, 3 * XP)])
    wait_bytes(rsem.at[17], gwbuf.at[pl.ds(0, 7 * YP)])
    wait_bytes(rsem.at[18], gwbuf.at[pl.ds(0, 7 * ZP)])
    wait_bytes(rsem.at[19], gwbuf.at[pl.ds(0, 3 * XP)])

    half = gwbuf.at[pl.ds(mine, HALF)]
    send(half, half, ssem, rsem, 20, at_core())
    pending.append((20, gwbuf.at[pl.ds(0, HALF)]))
    wait_bytes(rsem.at[20], gwbuf.at[pl.ds(0, HALF)])
    gw_copy = pltpu.make_async_copy(gwbuf.at[pl.ds(0, 27 * C)], gw_out, lsem.at[6])
    gw_copy.start()

    for stage, ref in pending:
        wait_bytes(ssem.at[stage], ref)
    for cp in feat_rim + dh_rim:
        cp.wait_send()
    gin_copy.wait()
    gw_copy.wait()


def on_device(feat_in, conv_out, activ, weight, gain, head, labels, grad_up):
    total_voxels = VOX * lax.axis_size("gx") * lax.axis_size("gy") * 1.0
    hbm = pl.BlockSpec(memory_space=pl.ANY)
    vmem = pl.BlockSpec(memory_space=pltpu.VMEM)
    V = pltpu.VMEM
    gin, gw, gg, sg = pl.pallas_call(
        functools.partial(kernel, total_voxels),
        out_shape=(
            jax.ShapeDtypeStruct((X, Y, Z, C), BF16),
            jax.ShapeDtypeStruct((27 * C, C), BF16),
            jax.ShapeDtypeStruct((1, C), F32),
            jax.ShapeDtypeStruct((1, C), F32),
        ),
        in_specs=[hbm, hbm, hbm, hbm, vmem, vmem, vmem, hbm],
        out_specs=(hbm, hbm, vmem, vmem),
        scratch_shapes=[
            V((X + 2, Y + 2, Z, C), BF16),
            V((X + 2, Y + 2, Z, C), BF16),
            V((X, Y, Z, C), BF16),
            V((X, Y, Z, C), BF16),
            V((X, Y, Z, C), BF16),
            V((27 * C, C), BF16),
            V((C, C), F32),
            V((VOX, C), F32),
            V((VOX, 3 * C), BF16),
            V((12 * C, PLANE), BF16),
            V((2 * HALF, C), CORE_T),
            V((X, Y, Z, C), BF16),
            V((2, 8, C), F32), V((4, 8, C), F32), V((8, 8, C), F32), V((8, 8, C), F32),
            V((HALF, C), CORE_T),
            V((HALF, C), BF16),
            V((8, YP, C), BF16), V((8, ZP, C), BF16), V((4, XP, C), BF16),
            V((8, YP // 8, C), F32), V((8, ZP // 8, C), F32), V((8, XP // 8, C), F32),
            V((4, YP // 8, C), F32), V((4, ZP // 8, C), F32), V((8, XP // 8, C), F32),
            V((8, YP // 8, C), F32), V((8, ZP // 8, C), F32), V((8, XP // 8, C), F32),
            V((8, YP // 8, C), F32), V((8, ZP // 8, C), F32), V((8, XP // 8, C), F32),
            V((2 * HALF, C), BF16),
            pltpu.SemaphoreType.DMA((7,)),
            pltpu.SemaphoreType.DMA((21,)),
            pltpu.SemaphoreType.DMA((21,)),
            pltpu.SemaphoreType.DMA((16,)),
            pltpu.SemaphoreType.DMA((16,)),
        ],
        compiler_params=pltpu.CompilerParams(
            collective_id=0, has_side_effects=True, vmem_limit_bytes=48 * 2**20
        ),
        name="conv_block_backward",
    )(feat_in, conv_out, activ, weight, gain.reshape(1, C), head, labels, grad_up)
    return gin, gw, gg.reshape(C), sg.reshape(C)


def solution(mesh):
    return jax.shard_map(
        on_device,
        mesh=mesh,
        in_specs=(
            P("gx", "gy", None, None),
            P("gx", "gy", None, None),
            P("gx", "gy", None, None),
            P(),
            P(),
            P(),
            P("gx", "gy", None),
            P("gx", "gy", None, None),
        ),
        out_specs=(P("gx", "gy", None, None), P(), P(), P()),
        check_vma=False,
    )
```

```python
import functools

import jax
import jax.numpy as jnp
from jax import lax
from jax.experimental import pallas as pl
from jax.experimental.pallas import tpu as pltpu
from jax.sharding import PartitionSpec as P

MESH = pl.DeviceIdType.MESH
F32 = jnp.float32
BF16 = jnp.bfloat16
C = 128
X, Y, Z = 2, 12, 32
COLS = X * Y
VOX = COLS * Z
PLANE = Y * Z
HALF = 14 * C
YP, ZP, XP = 64, 64, 192
YO, ZO, XO = 0, 8 * YP, 8 * YP + 8 * ZP
FULL = 12 * C
NT = (((1,), (1,)), ((), ()))
STATS = 4


def hops(k, n):
    return min(k, n - k)


def ring(n):
    return sorted(range(1, n), key=lambda k: -hops(k, n))


def kernel(
    total_voxels,
    feat, conv, activ, weight, gain, head, labels, grad_up,
    gin_out, gw_out, gg_out, sg_out,
    fpad, dpad, conv_v, dn_v, act_v, gu_v, w_v, lab_s, dhc_s, ft_s, h_s, gin_v,
    ra, rb,
    y1, z1, x1, y2, z2, x2, y3, z3, x3, y4, z4, x4, s2y, s2z, s2x, gwbuf,
    lsem, ssem, rsem,
):
    gx, gy = lax.axis_index("gx"), lax.axis_index("gy")
    z, xl, c = gx // 4, (gx // 2) % 2, gx % 2
    xh, y = gy // 8, gy % 8
    x = xh * 2 + xl

    def at(dx=0, dy=0, dz=0, dc=0):
        ax = (x + dx) % 4
        return (((z + dz) % 8) * 4 + (ax % 2) * 2 + (c + dc) % 2, (ax // 2) * 8 + (y + dy) % 8)

    other = at(dc=1)
    chip = gx // 2
    ahead, behind = (chip + 1) % 16, (chip + 15) % 16
    up_y, down_y = (gy + 1) % 16, (gy + 15) % 16
    up_x, down_x = (gx + 1) % 32, (gx + 31) % 32
    across = c * ahead + (1 - c) * behind

    yc = [(0, k, 0, e) for k in range(8) for e in range(2) if (k, e) != (0, 0)]
    xz = [(j, 0, k, 0) for j in range(4) for k in range(8) if (j, k) != (0, 0)]

    def far_first(offsets):
        return sorted(offsets, key=lambda o: -(hops(o[0], 4) + hops(o[1], 8) + hops(o[2], 8)))

    barrier = pltpu.get_barrier_semaphore()
    partners = [at(*o) for o in far_first(xz) + far_first(yc)]
    partners += [(i, j) for i in (behind * 2 + 1, ahead * 2) for j in (down_y, gy, up_y)]
    partners += [(chip * 2 + e, j) for j in (down_y, up_y) for e in range(2)]
    partners += [(i, j) for i in (down_x, up_x) for j in (down_y, gy, up_y)]
    for p in partners:
        pl.semaphore_signal(barrier, inc=1, device_id=p, device_id_type=MESH)

    own = 2 * c
    loads = [
        pltpu.make_async_copy(activ, act_v, lsem.at[0]),
        pltpu.make_async_copy(grad_up, gu_v, lsem.at[1]),
        pltpu.make_async_copy(conv, conv_v.at[pl.ds(own, X)], lsem.at[2]),
        pltpu.make_async_copy(feat, fpad.at[pl.ds(1 + own, X), pl.ds(1, Y)], lsem.at[3]),
        pltpu.make_async_copy(weight, w_v, lsem.at[4]),
    ]
    for cp in loads:
        cp.start()

    pending = []

    def send(stage, src, dst, dev):
        pltpu.make_async_remote_copy(
            src_ref=src, dst_ref=dst, send_sem=ssem.at[stage], recv_sem=rsem.at[stage],
            device_id=dev, device_id_type=MESH,
        ).start()

    def ring_sends(n, me, axis, src, dst):
        return [
            (hops(k, n), src((me + k) % n), dst(me), at(**{axis: k})) for k in ring(n)
        ]

    def start(stage, sends, count):
        for _, src, dst, dev in sends:
            send(stage, src, dst, dev)
        pending.append((stage, count))

    def wait_bytes(sem, ref):
        pltpu.make_async_copy(ref, ref, sem).wait()

    lab_s[...] = jnp.zeros_like(lab_s)
    for i in range(X):
        lab_s[pl.ds(16 * i, Y), pl.ds(0, Z)] = labels[:, i].astype(F32)
    lab_t = jnp.transpose(lab_s[...])[0:Z]

    row = lax.broadcasted_iota(jnp.int32, (C, C), 0)
    rep = jnp.zeros((C, C), F32)
    for k in range(3):
        rep = jnp.where(row % 3 == k, head[k : k + 1, :], rep)
    rep = jnp.where(row < 18, rep, 0.0)
    hi = rep.astype(BF16)
    left = rep - hi.astype(F32)
    mid = left.astype(BF16)
    low = (left - mid.astype(F32)).astype(BF16)
    part = row // 3
    back = jnp.where(
        (part == 0) | (part == 3) | (part == 5), hi.astype(F32),
        jnp.where((part == 1) | (part == 4), mid.astype(F32),
                  jnp.where(part == 2, low.astype(F32), 0.0)),
    ).astype(BF16)
    lane = lax.broadcasted_iota(jnp.int32, (VOX, C), 1)
    lane_class = (lane % 3).astype(F32)

    loads[0].wait()
    act = act_v[...].reshape(VOX, C)
    logits = (
        lax.dot_general(act, hi, NT, preferred_element_type=F32)
        + lax.dot_general(act, mid, NT, preferred_element_type=F32)
        + lax.dot_general(act, low, NT, preferred_element_type=F32)
    )
    label = jnp.concatenate(
        [
            jnp.broadcast_to(lab_t[:, 16 * i + j : 16 * i + j + 1], (Z, C))
            for i in range(X) for j in range(Y)
        ],
        axis=0,
    )
    dz = 0.5 * (jax.nn.sigmoid(logits) - (label == lane_class).astype(F32))
    dz_hi = dz.astype(BF16).astype(F32)
    dz_left = dz - dz_hi
    dz_mid = dz_left.astype(BF16).astype(F32)
    dz_low = dz_left - dz_mid
    spread = jnp.where(lane < 9, dz_hi, jnp.where(lane < 15, dz_mid, dz_low)).astype(BF16)
    loads[1].wait()
    ga = gu_v[...].reshape(VOX, C).astype(F32) + jnp.dot(
        spread, back, preferred_element_type=F32
    )
    dn = jnp.where(act.astype(F32) > 0, ga, 0.01 * ga)
    dn_v[pl.ds(own, X)] = dn.reshape(X, PLANE, C)
    loads[2].wait()
    h = conv_v[pl.ds(own, X)].reshape(VOX, C).astype(F32)
    stats = jnp.concatenate(
        [
            jnp.sum(jnp.sum(term.reshape(VOX // 8, 8, C), axis=0), axis=0, keepdims=True)
            for term in (h, h * h, dn, dn * h)
        ],
        axis=0,
    )

    slot_a = c * 8 + y
    ra[slot_a] = stats
    pl.semaphore_wait(barrier, len(partners))
    start(0, [(0, ra.at[slot_a], ra.at[slot_a], at(*o)) for o in far_first(yc)], ra.at[pl.ds(0, 15)])

    loads[3].wait()
    inner, edge = pl.ds(1, Y), 1 + own
    near = 1 + own + c
    far = 5 * (1 - c)
    planes = fpad.at[pl.ds(edge, X), inner]
    rim = [(0, planes, planes, other)]
    for e in range(2):
        rim.append((0, fpad.at[near, inner], fpad.at[far, inner], (across * 2 + e, gy)))
        for here, there, dev in ((Y, 0, up_y), (1, Y + 1, down_y)):
            rim.append(
                (0, fpad.at[pl.ds(edge, X), here], fpad.at[pl.ds(edge, X), there], (chip * 2 + e, dev))
            )
            rim.append((0, fpad.at[near, here], fpad.at[far, there], (across * 2 + e, dev)))
    rim_bytes = gwbuf.at[pl.ds(0, (6 * (Y + 2) - COLS) * Z)]
    start(1, rim, rim_bytes)
    mine = conv_v.at[pl.ds(own, X)]
    start(2, [(0, mine, mine, other)], conv_v.at[pl.ds(0, X)])
    mine = dn_v.at[pl.ds(own, X)]
    start(3, [(0, mine, mine, other)], dn_v.at[pl.ds(0, X)])

    wait_bytes(rsem.at[0], ra.at[pl.ds(0, 15)])
    slot_b = x * 8 + z
    rb[slot_b] = jnp.sum(ra[...], axis=0)
    start(4, [(0, rb.at[slot_b], rb.at[slot_b], at(*o)) for o in far_first(xz)], rb.at[pl.ds(0, 31)])

    wait_bytes(rsem.at[1], rim_bytes)

    def clear(cond, ref):
        @pl.when(cond)
        def _():
            ref[...] = jnp.zeros(ref.shape, BF16)

    clear(chip == 0, fpad.at[0])
    clear(chip == 15, fpad.at[5])
    clear(gy == 0, fpad.at[:, 0])
    clear(gy == 15, fpad.at[:, Y + 1])
    for pln in range(6):
        for b in range(3):
            block = jnp.transpose(fpad[pln, b : b + Y].reshape(PLANE, C))
            for a in range(3):
                if 0 <= pln - a < 4:
                    ft_s[(3 * a + b) * C : (3 * a + b + 1) * C, (pln - a) * PLANE : (pln - a + 1) * PLANE] = block
    loads[4].wait()
    wait_bytes(rsem.at[2], conv_v.at[pl.ds(0, X)])
    wait_bytes(rsem.at[3], dn_v.at[pl.ds(0, X)])

    wait_bytes(rsem.at[4], rb.at[pl.ds(0, 31)])
    stats = jnp.sum(rb[...], axis=0)
    mean = stats[0:1] / total_voxels
    rstd = lax.rsqrt(stats[1:2] / total_voxels - mean * mean + 1e-05)
    shift_grad = stats[2:3]
    gain_grad = rstd * (stats[3:4] - mean * shift_grad)
    scale = gain[...] * rstd
    shift_mean = shift_grad / total_voxels
    gain_mean = gain_grad / total_voxels

    zrow = lax.broadcasted_iota(jnp.int32, (PLANE, C), 0) % Z
    for p in range(4):
        hp = conv_v[p].reshape(PLANE, C).astype(F32)
        dh = scale * (dn_v[p] - shift_mean - (hp - mean) * rstd * gain_mean)
        rows = pl.ds(p * PLANE, PLANE)
        after = jnp.where(zrow == Z - 1, 0.0, pltpu.roll(dh, PLANE - 1, 0))
        before = jnp.where(zrow == 0, 0.0, pltpu.roll(dh, 1, 0))
        dhc_s[rows, 0:C] = after.astype(BF16)
        dhc_s[rows, C : 2 * C] = dh.astype(BF16)
        dhc_s[rows, 2 * C : 3 * C] = before.astype(BF16)

    def chunk(base, size):
        return lambda j: h_s.at[pl.ds(pl.multiple_of(base + j * size, 64), size)]

    block = jnp.dot(
        ft_s[pl.ds(pl.multiple_of(c * 7 * C, C), 2 * C)], dhc_s[...], preferred_element_type=F32
    ).astype(BF16)
    for f in range(2):
        for k in range(3):
            h_s[pl.ds((f * 3 + k) * C, C)] = block[f * C : (f + 1) * C, k * C : (k + 1) * C]
    start(5, ring_sends(8, y, "dy", chunk(YO, YP), lambda j: y1.at[j]), y1.at[pl.ds(0, 7)])
    block = jnp.dot(
        ft_s[pl.ds(pl.multiple_of(2 * C + c * 320, 64), 320)], dhc_s[...], preferred_element_type=F32
    ).astype(BF16)
    for j in range(5):
        tail = (1 - c) if j == 4 else (c if j == 0 else 0)
        q = j - c
        for k in range(3):
            at_row = tail * (FULL + k * 64) + (1 - tail) * ((2 + q // 2) * 3 * C + k * C + (q % 2) * 64)
            h_s[pl.ds(pl.multiple_of(at_row, 64), 64)] = block[j * 64 : (j + 1) * 64, k * C : (k + 1) * C]
    h_s[pl.ds(FULL + 192, 64)] = jnp.zeros((64, C), BF16)

    start(6, ring_sends(8, z, "dz", chunk(ZO, ZP), lambda j: z1.at[j]), z1.at[pl.ds(0, 7)])
    start(7, ring_sends(4, x, "dx", chunk(XO, XP), lambda j: x1.at[j]), x1.at[pl.ds(0, 3)])
    y1[y] = chunk(YO, YP)(y)[...]
    z1[z] = chunk(ZO, ZP)(z)[...]
    x1[x] = chunk(XO, XP)(x)[...]
    for i in range(X):
        rows = pl.ds(pl.multiple_of((own + i) * PLANE, PLANE), PLANE)
        dpad[1 + i, 1 : 1 + Y] = dhc_s[rows, C : 2 * C].reshape(Y, Z, C)
    gg_out[...] = gain_grad
    sg_out[...] = shift_grad

    def add_up(buf, n):
        acc = buf[0].astype(F32)
        for j in range(1, n):
            acc = acc + buf[j].astype(F32)
        return acc

    wait_bytes(rsem.at[5], y1.at[pl.ds(0, 7)])
    s2y[...] = add_up(y1, 8).reshape(8, YP // 8, C)
    y2[z] = s2y[z]
    start(8, ring_sends(8, z, "dz", lambda j: s2y.at[j], lambda j: y2.at[j]), y2.at[pl.ds(0, 7)])
    wait_bytes(rsem.at[6], z1.at[pl.ds(0, 7)])
    s2z[...] = add_up(z1, 8).reshape(8, ZP // 8, C)
    z2[y] = s2z[y]
    start(9, ring_sends(8, y, "dy", lambda j: s2z.at[j], lambda j: z2.at[j]), z2.at[pl.ds(0, 7)])
    wait_bytes(rsem.at[7], x1.at[pl.ds(0, 3)])
    s2x[...] = add_up(x1, 4).reshape(8, XP // 8, C)
    x2[y] = s2x[y]
    start(10, ring_sends(8, y, "dy", lambda j: s2x.at[j], lambda j: x2.at[j]), x2.at[pl.ds(0, 7)])

    inner_x = pl.ds(1, X)
    moves = [
        (X, inner, 0, inner, (up_x, gy)),
        (1, inner, X + 1, inner, (down_x, gy)),
        (inner_x, Y, inner_x, 0, (gx, up_y)),
        (inner_x, 1, inner_x, Y + 1, (gx, down_y)),
        (X, Y, 0, 0, (up_x, up_y)),
        (X, 1, 0, Y + 1, (up_x, down_y)),
        (1, Y, X + 1, 0, (down_x, up_y)),
        (1, 1, X + 1, Y + 1, (down_x, down_y)),
    ]
    dh_bytes = gwbuf.at[pl.ds(0, (4 * (Y + 2) - COLS) * Z)]
    start(11, [(0, dpad.at[a, b], dpad.at[d, e], dev) for a, b, d, e, dev in moves], dh_bytes)

    wait_bytes(rsem.at[10], x2.at[pl.ds(0, 7)])
    x3[z] = add_up(x2, 8)
    start(12, ring_sends(8, z, "dz", lambda j: x3.at[z], lambda j: x3.at[j]), x3.at[pl.ds(0, 7)])
    wait_bytes(rsem.at[8], y2.at[pl.ds(0, 7)])
    y3[x] = add_up(y2, 8)
    start(13, ring_sends(4, x, "dx", lambda j: y3.at[x], lambda j: y3.at[j]), y3.at[pl.ds(0, 3)])
    wait_bytes(rsem.at[9], z2.at[pl.ds(0, 7)])
    z3[x] = add_up(z2, 8)
    start(14, ring_sends(4, x, "dx", lambda j: z3.at[x], lambda j: z3.at[j]), z3.at[pl.ds(0, 3)])

    wait_bytes(rsem.at[11], dh_bytes)
    clear(gx == 0, dpad.at[0])
    clear(gx == 31, dpad.at[X + 1])
    clear(gy == 0, dpad.at[:, 0])
    clear(gy == 15, dpad.at[:, Y + 1])
    for i in range(X):
        total = jnp.zeros((PLANE, 3 * C), F32)
        for ab in range(9):
            a, b = ab // 3, ab % 3
            moved = dpad[i + 2 - a, 2 - b : 2 - b + Y].reshape(PLANE, C)
            total = total + lax.dot_general(
                moved, w_v[pl.ds(ab * 3 * C, 3 * C)], NT, preferred_element_type=F32
            )
        minus = jnp.where(zrow == Z - 1, 0.0, pltpu.roll(total[:, 0:C], PLANE - 1, 0))
        plus = jnp.where(zrow == 0, 0.0, pltpu.roll(total[:, 2 * C : 3 * C], 1, 0))
        gin_v[i] = (total[:, C : 2 * C] + minus + plus).astype(BF16).reshape(Y, Z, C)
    gin_copy = pltpu.make_async_copy(gin_v, gin_out, lsem.at[5])
    gin_copy.start()

    wait_bytes(rsem.at[13], y3.at[pl.ds(0, 3)])
    y4[z] = add_up(y3, 4)
    start(15, ring_sends(8, z, "dz", lambda j: y4.at[z], lambda j: y4.at[j]), y4.at[pl.ds(0, 7)])
    wait_bytes(rsem.at[14], z3.at[pl.ds(0, 3)])
    z4[y] = add_up(z3, 4)
    start(16, ring_sends(8, y, "dy", lambda j: z4.at[y], lambda j: z4.at[j]), z4.at[pl.ds(0, 7)])
    wait_bytes(rsem.at[12], x3.at[pl.ds(0, 7)])
    x4[y] = add_up(x3, 8)
    start(17, ring_sends(8, y, "dy", lambda j: x4.at[y], lambda j: x4.at[j]), x4.at[pl.ds(0, 7)])

    half = c * HALF

    def place(base, size):
        return lambda j: gwbuf.at[pl.ds(pl.multiple_of(half + base + j * size, 64), size)]

    place_y, place_z, place_x = place(YO, YP), place(ZO, ZP), place(XO, XP)
    wait_bytes(rsem.at[15], y4.at[pl.ds(0, 7)])
    place_y(y)[...] = y4[...].reshape(YP, C).astype(BF16)
    start(18, ring_sends(8, y, "dy", lambda j: place_y(y), place_y), gwbuf.at[pl.ds(0, 7 * YP)])
    wait_bytes(rsem.at[16], z4.at[pl.ds(0, 7)])
    place_z(z)[...] = z4[...].reshape(ZP, C).astype(BF16)
    start(19, ring_sends(8, z, "dz", lambda j: place_z(z), place_z), gwbuf.at[pl.ds(0, 7 * ZP)])
    wait_bytes(rsem.at[17], x4.at[pl.ds(0, 7)])
    place_x(x)[...] = x4[...].reshape(XP, C).astype(BF16)
    start(20, ring_sends(4, x, "dx", lambda j: place_x(x), place_x), gwbuf.at[pl.ds(0, 3 * XP)])

    parts = (
        (18, 21, 7 * YP, YO, 8 * YP), (19, 22, 7 * ZP, ZO, 8 * ZP), (20, 23, 3 * XP, XO, 4 * XP)
    )
    for stage, onward, arrived, base, size in parts:
        wait_bytes(rsem.at[stage], gwbuf.at[pl.ds(0, arrived)])
        ref = gwbuf.at[pl.ds(pl.multiple_of(half + base, 64), size)]
        start(onward, [(0, ref, ref, other)], gwbuf.at[pl.ds(0, size)])
    for _, onward, _, _, size in parts:
        wait_bytes(rsem.at[onward], gwbuf.at[pl.ds(0, size)])

    outs = [(0, 0, FULL), (HALF, 21 * C, 6 * C), (HALF + 6 * C, 15 * C, 6 * C)]
    for e in range(2):
        for k in range(3):
            outs.append((e * HALF + FULL + k * 64, FULL + k * C + e * 64, 64))
    copies = [
        pltpu.make_async_copy(gwbuf.at[pl.ds(a, n)], gw_out.at[pl.ds(b, n)], lsem.at[6 + i])
        for i, (a, b, n) in enumerate(outs)
    ]
    for cp in copies:
        cp.start()
    for stage, ref in pending:
        wait_bytes(ssem.at[stage], ref)
    gin_copy.wait()
    for cp in copies:
        cp.wait()


def copy_out(*refs):
    n = len(refs) // 3
    ins, outs, held, sem = refs[:n], refs[n : 2 * n], refs[2 * n : 3 * n], refs[-1]
    copies = [pltpu.make_async_copy(ins[i], held[i], sem.at[i]) for i in range(n)]
    for cp in copies:
        cp.start()
    back = [pltpu.make_async_copy(held[i], outs[i], sem.at[n + i]) for i in range(n)]
    for i in range(n):
        copies[i].wait()
        back[i].start()
    for cp in back:
        cp.wait()


def on_device(feat_in, conv_out, activ, weight, gain, head, labels, grad_up):
    total_voxels = VOX * lax.axis_size("gx") * lax.axis_size("gy") * 1.0
    hbm = pl.BlockSpec(memory_space=pltpu.HBM)
    anywhere = pl.BlockSpec(memory_space=pl.ANY)
    vmem = pl.BlockSpec(memory_space=pltpu.VMEM)
    V = pltpu.VMEM
    shapes = (
        jax.ShapeDtypeStruct((X, Y, Z, C), BF16),
        jax.ShapeDtypeStruct((27 * C, C), BF16),
        jax.ShapeDtypeStruct((1, C), F32),
        jax.ShapeDtypeStruct((1, C), F32),
    )
    outs = pl.pallas_call(
        functools.partial(kernel, total_voxels),
        out_shape=shapes,
        in_specs=[hbm, hbm, hbm, hbm, vmem, vmem, vmem, hbm],
        out_specs=(anywhere, anywhere, vmem, vmem),
        scratch_shapes=[
            V((6, Y + 2, Z, C), BF16),
            V((X + 2, Y + 2, Z, C), BF16),
            V((4, Y, Z, C), BF16),
            V((4, PLANE, C), F32),
            V((X, Y, Z, C), BF16),
            V((X, Y, Z, C), BF16),
            V((27 * C, C), BF16),
            V((C, C), F32),
            V((4 * PLANE, 3 * C), BF16),
            V((9 * C, 4 * PLANE), BF16),
            V((HALF, C), BF16),
            V((X, Y, Z, C), BF16),
            V((16, STATS, C), F32), V((32, STATS, C), F32),
            V((8, YP, C), BF16), V((8, ZP, C), BF16), V((4, XP, C), BF16),
            V((8, YP // 8, C), F32), V((8, ZP // 8, C), F32), V((8, XP // 8, C), F32),
            V((4, YP // 8, C), F32), V((4, ZP // 8, C), F32), V((8, XP // 8, C), F32),
            V((8, YP // 8, C), F32), V((8, ZP // 8, C), F32), V((8, XP // 8, C), F32),
            V((8, YP // 8, C), F32), V((8, ZP // 8, C), F32), V((8, XP // 8, C), F32),
            V((2 * HALF, C), BF16),
            pltpu.SemaphoreType.DMA((15,)),
            pltpu.SemaphoreType.DMA((24,)),
            pltpu.SemaphoreType.DMA((24,)),
        ],
        compiler_params=pltpu.CompilerParams(
            collective_id=0, has_side_effects=True, vmem_limit_bytes=58 * 2**20
        ),
        name="conv_block_backward",
    )(feat_in, conv_out, activ, weight, gain.reshape(1, C), head, labels.transpose(1, 0, 2), grad_up)
    gin, gw, gg, sg = pl.pallas_call(
        copy_out,
        out_shape=shapes,
        in_specs=[anywhere] * 4,
        out_specs=(hbm,) * 4,
        scratch_shapes=[V(t.shape, t.dtype) for t in shapes] + [pltpu.SemaphoreType.DMA((8,))],
        compiler_params=pltpu.CompilerParams(vmem_limit_bytes=60 * 2**20),
        name="copy_outputs",
    )(*outs)
    return gin, gw, gg.reshape(C), sg.reshape(C)


def solution(mesh):
    return jax.shard_map(
        on_device,
        mesh=mesh,
        in_specs=(
            P("gx", "gy", None, None),
            P("gx", "gy", None, None),
            P("gx", "gy", None, None),
            P(),
            P(),
            P(),
            P("gx", "gy", None),
            P("gx", "gy", None, None),
        ),
        out_specs=(P("gx", "gy", None, None), P(), P(), P()),
        check_vma=False,
    )
```

```python
import functools

import jax
import jax.numpy as jnp
from jax import lax
from jax.experimental import pallas as pl
from jax.experimental.pallas import tpu as pltpu
from jax.sharding import PartitionSpec as P

MESH = pl.DeviceIdType.MESH
F32 = jnp.float32
BF16 = jnp.bfloat16
C = 128
X, Y, Z = 2, 12, 32
COLS = X * Y
VOX = COLS * Z
PLANE = Y * Z
HALF = 14 * C
YP, ZP, XP = 64, 64, 192
YO, ZO, XO = 0, 8 * YP, 8 * YP + 8 * ZP
FULL = 12 * C
NT = (((1,), (1,)), ((), ()))
STATS = 4


def hops(k, n):
    return min(k, n - k)


def ring(n):
    return sorted(range(1, n), key=lambda k: -hops(k, n))


def kernel(
    total_voxels,
    feat, conv, activ, weight, gain_in, head_in, labels_in, grad_up,
    gin_out, gw_out, gg_out, sg_out,
    gain, head, labels, fpad, dpad, conv_v, dn_v, act_v, gu_v, w_v, lab_s, dhc_s, ft_s, h_s,
    ra, rb,
    y1, z1, x1, y2, z2, x2, y3, z3, x3, y4, z4, x4, s2y, s2z, s2x, gwbuf,
    lsem, ssem, rsem, gsem,
):
    gx, gy = lax.axis_index("gx"), lax.axis_index("gy")
    z, xl, c = gx // 4, (gx // 2) % 2, gx % 2
    xh, y = gy // 8, gy % 8
    x = xh * 2 + xl

    def at(dx=0, dy=0, dz=0, dc=0):
        ax = (x + dx) % 4
        return (((z + dz) % 8) * 4 + (ax % 2) * 2 + (c + dc) % 2, (ax // 2) * 8 + (y + dy) % 8)

    other = at(dc=1)
    chip = gx // 2
    ahead, behind = (chip + 1) % 16, (chip + 15) % 16
    up_y, down_y = (gy + 1) % 16, (gy + 15) % 16
    up_x, down_x = (gx + 1) % 32, (gx + 31) % 32
    across = c * ahead + (1 - c) * behind

    yc = [(0, k, 0, e) for k in range(8) for e in range(2) if (k, e) != (0, 0)]
    xz = [(j, 0, k, 0) for j in range(4) for k in range(8) if (j, k) != (0, 0)]

    def far_first(offsets):
        return sorted(offsets, key=lambda o: -(hops(o[0], 4) + hops(o[1], 8) + hops(o[2], 8)))

    own = 2 * c
    small = [
        pltpu.make_async_copy(labels_in, labels, lsem.at[6]),
        pltpu.make_async_copy(head_in, head, lsem.at[7]),
        pltpu.make_async_copy(gain_in, gain, lsem.at[8]),
    ]
    loads = [
        pltpu.make_async_copy(activ, act_v, lsem.at[0]),
        pltpu.make_async_copy(grad_up, gu_v, lsem.at[1]),
        pltpu.make_async_copy(conv, conv_v.at[pl.ds(own, X)], lsem.at[2]),
        pltpu.make_async_copy(feat, fpad.at[pl.ds(1 + own, X), pl.ds(1, Y)], lsem.at[3]),
        pltpu.make_async_copy(weight, w_v, lsem.at[4]),
    ]
    for cp in small + loads:
        cp.start()

    barrier = pltpu.get_barrier_semaphore()
    partners = [at(*o) for o in far_first(xz) + far_first(yc)]
    partners += [(i, j) for i in (behind * 2 + 1, ahead * 2) for j in (down_y, gy, up_y)]
    partners += [(chip * 2 + e, j) for j in (down_y, up_y) for e in range(2)]
    partners += [(i, j) for i in (down_x, up_x) for j in (down_y, gy, up_y)]
    for p in partners:
        pl.semaphore_signal(barrier, inc=1, device_id=p, device_id_type=MESH)

    pending = []

    def send(stage, src, dst, dev, arrival=None):
        pltpu.make_async_remote_copy(
            src_ref=src, dst_ref=dst, send_sem=ssem.at[stage],
            recv_sem=rsem.at[stage] if arrival is None else arrival,
            device_id=dev, device_id_type=MESH,
        ).start()

    def ring_sends(n, me, axis, src, dst):
        return [
            (hops(k, n), src((me + k) % n), dst(me), at(**{axis: k})) for k in ring(n)
        ]

    def start(stage, sends, count):
        for _, src, dst, dev in sends:
            send(stage, src, dst, dev)
        pending.append((stage, count))

    def wait_bytes(sem, ref):
        pltpu.make_async_copy(ref, ref, sem).wait()

    for cp in small:
        cp.wait()

    lab_s[...] = jnp.zeros_like(lab_s)
    for i in range(X):
        lab_s[pl.ds(16 * i, Y), pl.ds(0, Z)] = labels[:, i].astype(F32)
    lab_t = jnp.transpose(lab_s[...])[0:Z]

    row = lax.broadcasted_iota(jnp.int32, (C, C), 0)
    rep = jnp.zeros((C, C), F32)
    for k in range(3):
        rep = jnp.where(row % 3 == k, head[k : k + 1, :], rep)
    rep = jnp.where(row < 18, rep, 0.0)
    hi = rep.astype(BF16)
    left = rep - hi.astype(F32)
    mid = left.astype(BF16)
    low = (left - mid.astype(F32)).astype(BF16)
    part = row // 3
    back = jnp.where(
        (part == 0) | (part == 3) | (part == 5), hi.astype(F32),
        jnp.where((part == 1) | (part == 4), mid.astype(F32),
                  jnp.where(part == 2, low.astype(F32), 0.0)),
    ).astype(BF16)
    lane = lax.broadcasted_iota(jnp.int32, (1, C), 1)
    lane_class = (lane % 3).astype(F32)

    loads[0].wait()
    act = act_v[...].reshape(VOX, C)
    logits = (
        lax.dot_general(act, hi, NT, preferred_element_type=F32)
        + lax.dot_general(act, mid, NT, preferred_element_type=F32)
        + lax.dot_general(act, low, NT, preferred_element_type=F32)
    )
    label = jnp.concatenate(
        [
            jnp.broadcast_to(lab_t[:, 16 * i + j : 16 * i + j + 1], (Z, C))
            for i in range(X) for j in range(Y)
        ],
        axis=0,
    )
    dz = 0.5 * (jax.nn.sigmoid(logits) - (label == lane_class).astype(F32))
    dz_hi = dz.astype(BF16).astype(F32)
    dz_left = dz - dz_hi
    dz_mid = dz_left.astype(BF16).astype(F32)
    dz_low = dz_left - dz_mid
    spread = jnp.where(lane < 9, dz_hi, jnp.where(lane < 15, dz_mid, dz_low)).astype(BF16)
    loads[1].wait()
    ga = gu_v[...].reshape(VOX, C).astype(F32) + jnp.dot(
        spread, back, preferred_element_type=F32
    )
    dn = jnp.where(act.astype(F32) > 0, ga, 0.01 * ga)
    dn_v[pl.ds(own, X)] = dn.reshape(X, PLANE, C)
    loads[2].wait()
    h = conv_v[pl.ds(own, X)].reshape(VOX, C).astype(F32)
    stats = jnp.concatenate(
        [
            jnp.sum(jnp.sum(term.reshape(VOX // 8, 8, C), axis=0), axis=0, keepdims=True)
            for term in (h, h * h, dn, dn * h)
        ],
        axis=0,
    )

    slot_a = c * 8 + y
    ra[slot_a] = stats
    pl.semaphore_wait(barrier, len(partners))
    start(0, [(0, ra.at[slot_a], ra.at[slot_a], at(*o)) for o in far_first(yc)], ra.at[pl.ds(0, 15)])

    loads[3].wait()
    inner, edge = pl.ds(1, Y), 1 + own
    near = 1 + own + c
    far = 5 * (1 - c)
    planes = fpad.at[pl.ds(edge, X), inner]
    rim = [(0, planes, planes, other)]
    for e in range(2):
        rim.append((0, fpad.at[near, inner], fpad.at[far, inner], (across * 2 + e, gy)))
        for here, there, dev in ((Y, 0, up_y), (1, Y + 1, down_y)):
            rim.append(
                (0, fpad.at[pl.ds(edge, X), here], fpad.at[pl.ds(edge, X), there], (chip * 2 + e, dev))
            )
            rim.append((0, fpad.at[near, here], fpad.at[far, there], (across * 2 + e, dev)))
    rim_bytes = gwbuf.at[pl.ds(0, (6 * (Y + 2) - COLS) * Z)]
    start(1, rim, rim_bytes)
    mine = conv_v.at[pl.ds(own, X)]
    start(2, [(0, mine, mine, other)], conv_v.at[pl.ds(0, X)])
    mine = dn_v.at[pl.ds(own, X)]
    start(3, [(0, mine, mine, other)], dn_v.at[pl.ds(0, X)])

    wait_bytes(rsem.at[0], ra.at[pl.ds(0, 15)])
    slot_b = x * 8 + z
    rb[slot_b] = jnp.sum(ra[...], axis=0)
    start(4, [(0, rb.at[slot_b], rb.at[slot_b], at(*o)) for o in far_first(xz)], rb.at[pl.ds(0, 31)])

    wait_bytes(rsem.at[1], rim_bytes)

    def clear(cond, ref):
        @pl.when(cond)
        def _():
            ref[...] = jnp.zeros(ref.shape, BF16)

    clear(chip == 0, fpad.at[0])
    clear(chip == 15, fpad.at[5])
    clear(gy == 0, fpad.at[:, 0])
    clear(gy == 15, fpad.at[:, Y + 1])
    for pln in range(6):
        for b in range(3):
            block = jnp.transpose(fpad[pln, b : b + Y].reshape(PLANE, C))
            for a in range(3):
                if 0 <= pln - a < 4:
                    ft_s[(3 * a + b) * C : (3 * a + b + 1) * C, (pln - a) * PLANE : (pln - a + 1) * PLANE] = block
    loads[4].wait()
    wait_bytes(rsem.at[2], conv_v.at[pl.ds(0, X)])
    wait_bytes(rsem.at[3], dn_v.at[pl.ds(0, X)])

    wait_bytes(rsem.at[4], rb.at[pl.ds(0, 31)])
    stats = jnp.sum(rb[...], axis=0)
    mean = stats[0:1] / total_voxels
    rstd = lax.rsqrt(stats[1:2] / total_voxels - mean * mean + 1e-05)
    shift_grad = stats[2:3]
    gain_grad = rstd * (stats[3:4] - mean * shift_grad)
    scale = gain[...] * rstd
    shift_mean = shift_grad / total_voxels
    gain_mean = gain_grad / total_voxels

    zrow = lax.broadcasted_iota(jnp.int32, (PLANE, C), 0) & (Z - 1)
    for p in range(4):
        hp = conv_v[p].reshape(PLANE, C).astype(F32)
        dh = scale * (dn_v[p] - shift_mean - (hp - mean) * rstd * gain_mean)
        rows = pl.ds(p * PLANE, PLANE)
        after = jnp.where(zrow == Z - 1, 0.0, pltpu.roll(dh, PLANE - 1, 0))
        before = jnp.where(zrow == 0, 0.0, pltpu.roll(dh, 1, 0))
        dhc_s[rows, 0:C] = after.astype(BF16)
        dhc_s[rows, C : 2 * C] = dh.astype(BF16)
        dhc_s[rows, 2 * C : 3 * C] = before.astype(BF16)

    def chunk(base, size):
        return lambda j: h_s.at[pl.ds(pl.multiple_of(base + j * size, 64), size)]

    block = jnp.dot(
        ft_s[pl.ds(pl.multiple_of(c * 6 * C, C), 3 * C)], dhc_s[...], preferred_element_type=F32
    ).astype(BF16)
    for f in range(3):
        for k in range(3):
            h_s[pl.ds((f * 3 + k) * C, C)] = block[f * C : (f + 1) * C, k * C : (k + 1) * C]
    first = ring_sends(8, y, "dy", chunk(YO, YP), lambda j: y1.at[j])
    second = ring_sends(8, z, "dz", chunk(ZO, ZP), lambda j: z1.at[j])
    for sy, sz in zip(first, second):
        send(5, *sy[1:])
        send(6, *sz[1:])
    pending.append((5, y1.at[pl.ds(0, 7)]))
    pending.append((6, z1.at[pl.ds(0, 7)]))
    block = jnp.dot(
        ft_s[pl.ds(pl.multiple_of(3 * C + c * 192, 64), 192)], dhc_s[...], preferred_element_type=F32
    ).astype(BF16)
    for j in range(3):
        tail = (1 - c) if j == 2 else (c if j == 0 else 0)
        for k in range(3):
            at_row = tail * (FULL + k * 64) + (1 - tail) * (9 * C + k * C + (j - c) * 64)
            h_s[pl.ds(pl.multiple_of(at_row, 64), 64)] = block[j * 64 : (j + 1) * 64, k * C : (k + 1) * C]
    h_s[pl.ds(FULL + 192, 64)] = jnp.zeros((64, C), BF16)

    start(7, ring_sends(4, x, "dx", chunk(XO, XP), lambda j: x1.at[j]), x1.at[pl.ds(0, 3)])
    y1[y] = chunk(YO, YP)(y)[...]
    z1[z] = chunk(ZO, ZP)(z)[...]
    x1[x] = chunk(XO, XP)(x)[...]
    for i in range(X):
        rows = pl.ds(pl.multiple_of((own + i) * PLANE, PLANE), PLANE)
        dpad[1 + i, 1 : 1 + Y] = dhc_s[rows, C : 2 * C].reshape(Y, Z, C)
    gg_out[...] = gain_grad
    sg_out[...] = shift_grad

    def add_up(buf, n):
        acc = buf[0].astype(F32)
        for j in range(1, n):
            acc = acc + buf[j].astype(F32)
        return acc

    wait_bytes(rsem.at[5], y1.at[pl.ds(0, 7)])
    s2y[...] = add_up(y1, 8).reshape(8, YP // 8, C)
    y2[z] = s2y[z]
    start(8, ring_sends(8, z, "dz", lambda j: s2y.at[j], lambda j: y2.at[j]), y2.at[pl.ds(0, 7)])
    wait_bytes(rsem.at[6], z1.at[pl.ds(0, 7)])
    s2z[...] = add_up(z1, 8).reshape(8, ZP // 8, C)
    z2[y] = s2z[y]
    start(9, ring_sends(8, y, "dy", lambda j: s2z.at[j], lambda j: z2.at[j]), z2.at[pl.ds(0, 7)])
    wait_bytes(rsem.at[7], x1.at[pl.ds(0, 3)])
    s2x[...] = add_up(x1, 4).reshape(8, XP // 8, C)
    x2[y] = s2x[y]
    start(10, ring_sends(8, y, "dy", lambda j: s2x.at[j], lambda j: x2.at[j]), x2.at[pl.ds(0, 7)])

    inner_x = pl.ds(1, X)
    moves = [
        (X, inner, 0, inner, (up_x, gy)),
        (1, inner, X + 1, inner, (down_x, gy)),
        (inner_x, Y, inner_x, 0, (gx, up_y)),
        (inner_x, 1, inner_x, Y + 1, (gx, down_y)),
        (X, Y, 0, 0, (up_x, up_y)),
        (X, 1, 0, Y + 1, (up_x, down_y)),
        (1, Y, X + 1, 0, (down_x, up_y)),
        (1, 1, X + 1, Y + 1, (down_x, down_y)),
    ]
    dh_bytes = gwbuf.at[pl.ds(0, (4 * (Y + 2) - COLS) * Z)]
    start(11, [(0, dpad.at[a, b], dpad.at[d, e], dev) for a, b, d, e, dev in moves], dh_bytes)

    wait_bytes(rsem.at[10], x2.at[pl.ds(0, 7)])
    x3[z] = add_up(x2, 8)
    start(12, ring_sends(8, z, "dz", lambda j: x3.at[z], lambda j: x3.at[j]), x3.at[pl.ds(0, 7)])
    wait_bytes(rsem.at[8], y2.at[pl.ds(0, 7)])
    y3[x] = add_up(y2, 8)
    start(13, ring_sends(4, x, "dx", lambda j: y3.at[x], lambda j: y3.at[j]), y3.at[pl.ds(0, 3)])
    wait_bytes(rsem.at[9], z2.at[pl.ds(0, 7)])
    z3[x] = add_up(z2, 8)
    start(14, ring_sends(4, x, "dx", lambda j: z3.at[x], lambda j: z3.at[j]), z3.at[pl.ds(0, 3)])

    wait_bytes(rsem.at[11], dh_bytes)
    clear(gx == 0, dpad.at[0])
    clear(gx == 31, dpad.at[X + 1])
    clear(gy == 0, dpad.at[:, 0])
    clear(gy == 15, dpad.at[:, Y + 1])
    for i in range(X):
        total = jnp.zeros((PLANE, 3 * C), F32)
        for ab in range(9):
            a, b = ab // 3, ab % 3
            moved = dpad[i + 2 - a, 2 - b : 2 - b + Y].reshape(PLANE, C)
            total = total + lax.dot_general(
                moved, w_v[pl.ds(ab * 3 * C, 3 * C)], NT, preferred_element_type=F32
            )
        minus = jnp.where(zrow == Z - 1, 0.0, pltpu.roll(total[:, 0:C], PLANE - 1, 0))
        plus = jnp.where(zrow == 0, 0.0, pltpu.roll(total[:, 2 * C : 3 * C], 1, 0))
        gin_out[i] = (total[:, C : 2 * C] + minus + plus).astype(BF16).reshape(Y, Z, C)

    wait_bytes(rsem.at[13], y3.at[pl.ds(0, 3)])
    y4[z] = add_up(y3, 4)
    start(15, ring_sends(8, z, "dz", lambda j: y4.at[z], lambda j: y4.at[j]), y4.at[pl.ds(0, 7)])
    wait_bytes(rsem.at[14], z3.at[pl.ds(0, 3)])
    z4[y] = add_up(z3, 4)
    start(16, ring_sends(8, y, "dy", lambda j: z4.at[y], lambda j: z4.at[j]), z4.at[pl.ds(0, 7)])
    wait_bytes(rsem.at[12], x3.at[pl.ds(0, 7)])
    x4[y] = add_up(x3, 8)
    start(17, ring_sends(8, y, "dy", lambda j: x4.at[y], lambda j: x4.at[j]), x4.at[pl.ds(0, 7)])

    half, half_other = c * HALF, (1 - c) * HALF
    spans = (
        (15, y4, 18, 21, 8, y, "dy", YO, YP), (16, z4, 19, 22, 8, z, "dz", ZO, ZP),
        (17, x4, 20, 23, 4, x, "dx", XO, XP),
    )

    def place(base, j, size):
        return gwbuf.at[pl.ds(pl.multiple_of(half + base + j * size, 64), size)]

    for stage, buf, out, onward, n, me, axis, base, size in spans:
        wait_bytes(rsem.at[stage], buf.at[pl.ds(0, 7)])
        ref = place(base, me, size)
        ref[...] = buf[...].reshape(size, C).astype(BF16)
        for k in ring(n):
            send(out, ref, ref, at(**{axis: k}), gsem.at[out - 18, k])
        pending.append((out, gwbuf.at[pl.ds(0, (n - 1) * size)]))
    for stage, buf, out, onward, n, me, axis, base, size in spans:
        ref = place(base, me, size)
        send(onward, ref, ref, other)
        pending.append((onward, gwbuf.at[pl.ds(0, n * size)]))
    for far in range(1, 5):
        for stage, buf, out, onward, n, me, axis, base, size in spans:
            for k in range(1, n):
                if hops(k, n) == far:
                    ref = place(base, (me - k) % n, size)
                    wait_bytes(gsem.at[out - 18, k], ref)
                    send(onward, ref, ref, other)

    def write_half(core, base):
        moves = [(t * C, core * 18 * C + t * C, C) for t in range(9)]
        moves += [(t * C, core * 6 * C + t * C, C) for t in range(9, 12)]
        moves += [(FULL + k * 64, FULL + k * C + core * 64, 64) for k in range(3)]
        for src, dst, n in moves:
            gw_out[pl.ds(pl.multiple_of(dst, 64), n)] = gwbuf[pl.ds(pl.multiple_of(base + src, 64), n)]

    write_half(c, half)
    for _, _, _, onward, n, _, _, _, size in spans:
        wait_bytes(rsem.at[onward], gwbuf.at[pl.ds(0, n * size)])
    write_half(1 - c, half_other)
    for stage, ref in pending:
        wait_bytes(ssem.at[stage], ref)


def copy_out(*refs):
    n = len(refs) // 2
    ins, outs, sem = refs[:n], refs[n : 2 * n], refs[-1]
    copies = [pltpu.make_async_copy(ins[i], outs[i], sem.at[i]) for i in range(n)]
    for cp in copies:
        cp.start()
    for cp in copies:
        cp.wait()


def on_device(feat_in, conv_out, activ, weight, gain, head, labels, grad_up):
    total_voxels = VOX * lax.axis_size("gx") * lax.axis_size("gy") * 1.0
    hbm = pl.BlockSpec(memory_space=pltpu.HBM)
    anywhere = pl.BlockSpec(memory_space=pl.ANY)
    vmem = pl.BlockSpec(memory_space=pltpu.VMEM)
    V = pltpu.VMEM
    shapes = (
        jax.ShapeDtypeStruct((X, Y, Z, C), BF16),
        jax.ShapeDtypeStruct((27 * C, C), BF16),
        jax.ShapeDtypeStruct((1, C), F32),
        jax.ShapeDtypeStruct((1, C), F32),
    )
    operands = (
        feat_in, conv_out, activ, weight, gain.reshape(1, C), head, labels.transpose(1, 0, 2), grad_up
    )
    operands = [pltpu.with_memory_space_constraint(t, pltpu.HBM) for t in operands]
    outs = pl.pallas_call(
        functools.partial(kernel, total_voxels),
        out_shape=shapes,
        in_specs=[hbm] * 8,
        out_specs=(vmem,) * 4,
        scratch_shapes=[
            V((1, C), F32),
            V((3, C), F32),
            V((Y, X, Z), jnp.int32),
            V((6, Y + 2, Z, C), BF16),
            V((X + 2, Y + 2, Z, C), BF16),
            V((4, Y, Z, C), BF16),
            V((4, PLANE, C), F32),
            V((X, Y, Z, C), BF16),
            V((X, Y, Z, C), BF16),
            V((27 * C, C), BF16),
            V((C, C), F32),
            V((4 * PLANE, 3 * C), BF16),
            V((9 * C, 4 * PLANE), BF16),
            V((HALF, C), BF16),
            V((16, STATS, C), F32), V((32, STATS, C), F32),
            V((8, YP, C), BF16), V((8, ZP, C), BF16), V((4, XP, C), BF16),
            V((8, YP // 8, C), F32), V((8, ZP // 8, C), F32), V((8, XP // 8, C), F32),
            V((4, YP // 8, C), F32), V((4, ZP // 8, C), F32), V((8, XP // 8, C), F32),
            V((8, YP // 8, C), F32), V((8, ZP // 8, C), F32), V((8, XP // 8, C), F32),
            V((8, YP // 8, C), F32), V((8, ZP // 8, C), F32), V((8, XP // 8, C), F32),
            V((2 * HALF, C), BF16),
            pltpu.SemaphoreType.DMA((9,)),
            pltpu.SemaphoreType.DMA((24,)),
            pltpu.SemaphoreType.DMA((24,)),
            pltpu.SemaphoreType.DMA((3, 8)),
        ],
        compiler_params=pltpu.CompilerParams(
            collective_id=0, has_side_effects=True, vmem_limit_bytes=40 * 2**20
        ),
        name="conv_block_backward",
    )(*operands)
    gin, gw, gg, sg = pl.pallas_call(
        copy_out,
        out_shape=shapes,
        in_specs=[anywhere] * 4,
        out_specs=(hbm,) * 4,
        scratch_shapes=[pltpu.SemaphoreType.DMA((4,))],
        compiler_params=pltpu.CompilerParams(vmem_limit_bytes=4 * 2**20),
        name="copy_outputs",
    )(*outs)
    return gin, gw, gg.reshape(C), sg.reshape(C)


def solution(mesh):
    return jax.shard_map(
        on_device,
        mesh=mesh,
        in_specs=(
            P("gx", "gy", None, None),
            P("gx", "gy", None, None),
            P("gx", "gy", None, None),
            P(),
            P(),
            P(),
            P("gx", "gy", None),
            P("gx", "gy", None, None),
        ),
        out_specs=(P("gx", "gy", None, None), P(), P(), P()),
        check_vma=False,
    )
```

```python
import functools

import jax
import jax.numpy as jnp
from jax import lax
from jax.experimental import pallas as pl
from jax.experimental.pallas import tpu as pltpu
from jax.sharding import PartitionSpec as P

MESH = pl.DeviceIdType.MESH
F32 = jnp.float32
BF16 = jnp.bfloat16
C = 128
X, Y, Z = 2, 12, 32
COLS = X * Y
VOX = COLS * Z
PLANE = Y * Z
HALF = 14 * C
YP, ZP, XP = 64, 64, 192
YO, ZO, XO = 0, 8 * YP, 8 * YP + 8 * ZP
FULL = 12 * C
NT = (((1,), (1,)), ((), ()))
STATS = 4


def hops(k, n):
    return min(k, n - k)


def ring(n):
    return sorted(range(1, n), key=lambda k: -hops(k, n))


def kernel(
    total_voxels,
    feat, conv, activ, weight, gain_in, head_in, labels_in, grad_up,
    gin_out, gw_out, gg_out, sg_out,
    gain, head, labels, fpad, dpad, conv_v, dn_v, act_v, gu_v, w_v, lab_s, dhc_s, ft_s, h_s,
    ra, rb,
    y1, z1, x1, y2, z2, x2, y3, z3, x3, y4, z4, x4, s2y, s2z, s2x, gwbuf,
    lsem, ssem, rsem, late,
):
    gx, gy = lax.axis_index("gx"), lax.axis_index("gy")
    z, xl, c = gx // 4, (gx // 2) % 2, gx % 2
    xh, y = gy // 8, gy % 8
    x = xh * 2 + xl

    def at(dx=0, dy=0, dz=0, dc=0):
        ax = (x + dx) % 4
        return (((z + dz) % 8) * 4 + (ax % 2) * 2 + (c + dc) % 2, (ax // 2) * 8 + (y + dy) % 8)

    other = at(dc=1)
    chip = gx // 2
    ahead, behind = (chip + 1) % 16, (chip + 15) % 16
    up_y, down_y = (gy + 1) % 16, (gy + 15) % 16
    up_x, down_x = (gx + 1) % 32, (gx + 31) % 32
    across = c * ahead + (1 - c) * behind

    yc = [(0, k, 0, e) for k in range(8) for e in range(2) if (k, e) != (0, 0)]
    xz = [(j, 0, k, 0) for j in range(4) for k in range(8) if (j, k) != (0, 0)]

    def far_first(offsets):
        return sorted(offsets, key=lambda o: -(hops(o[0], 4) + hops(o[1], 8) + hops(o[2], 8)))

    barrier = pltpu.get_barrier_semaphore()

    def signal(sem, dev):
        pl.semaphore_signal(sem, inc=1, device_id=dev, device_id_type=MESH)

    rank = z * 4 + x

    def rank_of(o):
        return ((z + o[2]) % 8) * 4 + (x + o[0]) % 4

    partners = [at(*o) for o in far_first(yc)]
    partners += [(i, j) for i in (behind * 2 + 1, ahead * 2) for j in (down_y, gy, up_y)]
    partners += [(chip * 2 + e, j) for j in (down_y, up_y) for e in range(2)]
    partners += [(i, j) for i in (down_x, up_x) for j in (down_y, gy, up_y)]
    for p in partners[:15]:
        signal(barrier, p)

    own = 2 * c
    small = [
        pltpu.make_async_copy(labels_in, labels, lsem.at[6]),
        pltpu.make_async_copy(head_in, head, lsem.at[7]),
        pltpu.make_async_copy(gain_in, gain, lsem.at[8]),
    ]
    loads = [
        pltpu.make_async_copy(activ, act_v, lsem.at[0]),
        pltpu.make_async_copy(grad_up, gu_v, lsem.at[1]),
        pltpu.make_async_copy(conv, conv_v.at[pl.ds(own, X)], lsem.at[2]),
        pltpu.make_async_copy(feat, fpad.at[pl.ds(1 + own, X), pl.ds(1, Y)], lsem.at[3]),
        pltpu.make_async_copy(weight, w_v, lsem.at[4]),
    ]
    for cp in small + loads:
        cp.start()

    for p in partners[15:]:
        signal(barrier, p)
    for o in far_first(xz):
        @pl.when(rank_of(o) > rank)
        def _():
            signal(barrier, at(*o))

    pending = []

    def send(stage, src, dst, dev):
        pltpu.make_async_remote_copy(
            src_ref=src, dst_ref=dst, send_sem=ssem.at[stage], recv_sem=rsem.at[stage],
            device_id=dev, device_id_type=MESH,
        ).start()

    def ring_sends(n, me, axis, src, dst):
        return [
            (hops(k, n), src((me + k) % n), dst(me), at(**{axis: k})) for k in ring(n)
        ]

    def start(stage, sends, count):
        for _, src, dst, dev in sends:
            send(stage, src, dst, dev)
        pending.append((stage, count))

    def wait_bytes(sem, ref):
        pltpu.make_async_copy(ref, ref, sem).wait()

    for cp in small:
        cp.wait()

    lab_s[...] = jnp.zeros_like(lab_s)
    for i in range(X):
        lab_s[pl.ds(16 * i, Y), pl.ds(0, Z)] = labels[:, i].astype(F32)
    lab_t = jnp.transpose(lab_s[...])[0:Z]

    row = lax.broadcasted_iota(jnp.int32, (C, C), 0)
    rep = jnp.zeros((C, C), F32)
    for k in range(3):
        rep = jnp.where(row % 3 == k, head[k : k + 1, :], rep)
    rep = jnp.where(row < 18, rep, 0.0)
    hi = rep.astype(BF16)
    left = rep - hi.astype(F32)
    mid = left.astype(BF16)
    low = (left - mid.astype(F32)).astype(BF16)
    part = row // 3
    back = jnp.where(
        (part == 0) | (part == 3) | (part == 5), hi.astype(F32),
        jnp.where((part == 1) | (part == 4), mid.astype(F32),
                  jnp.where(part == 2, low.astype(F32), 0.0)),
    ).astype(BF16)
    lane = lax.broadcasted_iota(jnp.int32, (1, C), 1)
    lane_class = (lane % 3).astype(F32)

    loads[0].wait()
    act = act_v[...].reshape(VOX, C)
    logits = (
        lax.dot_general(act, hi, NT, preferred_element_type=F32)
        + lax.dot_general(act, mid, NT, preferred_element_type=F32)
        + lax.dot_general(act, low, NT, preferred_element_type=F32)
    )
    label = jnp.concatenate(
        [
            jnp.broadcast_to(lab_t[:, 16 * i + j : 16 * i + j + 1], (Z, C))
            for i in range(X) for j in range(Y)
        ],
        axis=0,
    )
    dz = 0.5 * (jax.nn.sigmoid(logits) - (label == lane_class).astype(F32))
    dz_hi = dz.astype(BF16).astype(F32)
    dz_left = dz - dz_hi
    dz_mid = dz_left.astype(BF16).astype(F32)
    dz_low = dz_left - dz_mid
    spread = jnp.where(lane < 9, dz_hi, jnp.where(lane < 15, dz_mid, dz_low)).astype(BF16)
    loads[1].wait()
    ga = gu_v[...].reshape(VOX, C).astype(F32) + jnp.dot(
        spread, back, preferred_element_type=F32
    )
    dn = jnp.where(act.astype(F32) > 0, ga, 0.01 * ga)
    dn_v[pl.ds(own, X)] = dn.reshape(X, PLANE, C)
    loads[2].wait()
    h = conv_v[pl.ds(own, X)].reshape(VOX, C).astype(F32)
    stats = jnp.concatenate(
        [
            jnp.sum(jnp.sum(term.reshape(VOX // 8, 8, C), axis=0), axis=0, keepdims=True)
            for term in (h, h * h, dn, dn * h)
        ],
        axis=0,
    )

    slot_a = c * 8 + y
    ra[slot_a] = stats
    pl.semaphore_wait(barrier, len(partners) + rank)
    start(0, [(0, ra.at[slot_a], ra.at[slot_a], at(*o)) for o in far_first(yc)], ra.at[pl.ds(0, 15)])

    for o in far_first(xz):
        @pl.when(rank_of(o) < rank)
        def _():
            signal(late, at(*o))

    loads[3].wait()
    inner, edge = pl.ds(1, Y), 1 + own
    near = 1 + own + c
    far = 5 * (1 - c)
    planes = fpad.at[pl.ds(edge, X), inner]
    rim = [(0, planes, planes, other)]
    for e in range(2):
        rim.append((0, fpad.at[near, inner], fpad.at[far, inner], (across * 2 + e, gy)))
        for here, there, dev in ((Y, 0, up_y), (1, Y + 1, down_y)):
            rim.append(
                (0, fpad.at[pl.ds(edge, X), here], fpad.at[pl.ds(edge, X), there], (chip * 2 + e, dev))
            )
            rim.append((0, fpad.at[near, here], fpad.at[far, there], (across * 2 + e, dev)))
    rim_bytes = gwbuf.at[pl.ds(0, (6 * (Y + 2) - COLS) * Z)]
    start(1, rim, rim_bytes)
    mine = conv_v.at[pl.ds(own, X)]
    start(2, [(0, mine, mine, other)], conv_v.at[pl.ds(0, X)])
    mine = dn_v.at[pl.ds(own, X)]
    start(3, [(0, mine, mine, other)], dn_v.at[pl.ds(0, X)])

    wait_bytes(rsem.at[0], ra.at[pl.ds(0, 15)])
    slot_b = x * 8 + z
    rb[slot_b] = jnp.sum(ra[...], axis=0)

    @pl.when(rank < 31)
    def _():
        pl.semaphore_wait(late, 31 - rank)

    start(4, [(0, rb.at[slot_b], rb.at[slot_b], at(*o)) for o in far_first(xz)], rb.at[pl.ds(0, 31)])

    wait_bytes(rsem.at[1], rim_bytes)

    def clear(cond, ref):
        @pl.when(cond)
        def _():
            ref[...] = jnp.zeros(ref.shape, BF16)

    clear(chip == 0, fpad.at[0])
    clear(chip == 15, fpad.at[5])
    clear(gy == 0, fpad.at[:, 0])
    clear(gy == 15, fpad.at[:, Y + 1])
    for pln in range(6):
        for b in range(3):
            block = jnp.transpose(fpad[pln, b : b + Y].reshape(PLANE, C))
            for a in range(3):
                if 0 <= pln - a < 4:
                    ft_s[(3 * a + b) * C : (3 * a + b + 1) * C, (pln - a) * PLANE : (pln - a + 1) * PLANE] = block
    loads[4].wait()
    wait_bytes(rsem.at[2], conv_v.at[pl.ds(0, X)])
    wait_bytes(rsem.at[3], dn_v.at[pl.ds(0, X)])

    wait_bytes(rsem.at[4], rb.at[pl.ds(0, 31)])
    stats = jnp.sum(rb[...], axis=0)
    mean = stats[0:1] / total_voxels
    rstd = lax.rsqrt(stats[1:2] / total_voxels - mean * mean + 1e-05)
    shift_grad = stats[2:3]
    gain_grad = rstd * (stats[3:4] - mean * shift_grad)
    scale = gain[...] * rstd
    shift_mean = shift_grad / total_voxels
    gain_mean = gain_grad / total_voxels

    zrow = lax.broadcasted_iota(jnp.int32, (PLANE, C), 0) & (Z - 1)
    for p in range(4):
        hp = conv_v[p].reshape(PLANE, C).astype(F32)
        dh = scale * (dn_v[p] - shift_mean - (hp - mean) * rstd * gain_mean)
        rows = pl.ds(p * PLANE, PLANE)
        after = jnp.where(zrow == Z - 1, 0.0, pltpu.roll(dh, PLANE - 1, 0))
        before = jnp.where(zrow == 0, 0.0, pltpu.roll(dh, 1, 0))
        dhc_s[rows, 0:C] = after.astype(BF16)
        dhc_s[rows, C : 2 * C] = dh.astype(BF16)
        dhc_s[rows, 2 * C : 3 * C] = before.astype(BF16)

    def chunk(base, size):
        return lambda j: h_s.at[pl.ds(pl.multiple_of(base + j * size, 64), size)]

    block = jnp.dot(
        ft_s[pl.ds(pl.multiple_of(c * 6 * C, C), 3 * C)], dhc_s[...], preferred_element_type=F32
    ).astype(BF16)
    for f in range(3):
        for k in range(3):
            h_s[pl.ds((f * 3 + k) * C, C)] = block[f * C : (f + 1) * C, k * C : (k + 1) * C]
    first = ring_sends(8, y, "dy", chunk(YO, YP), lambda j: y1.at[j])
    second = ring_sends(8, z, "dz", chunk(ZO, ZP), lambda j: z1.at[j])
    for sy, sz in zip(first, second):
        send(5, *sy[1:])
        send(6, *sz[1:])
    pending.append((5, y1.at[pl.ds(0, 7)]))
    pending.append((6, z1.at[pl.ds(0, 7)]))
    block = jnp.dot(
        ft_s[pl.ds(pl.multiple_of(3 * C + c * 192, 64), 192)], dhc_s[...], preferred_element_type=F32
    ).astype(BF16)
    for j in range(3):
        tail = (1 - c) if j == 2 else (c if j == 0 else 0)
        for k in range(3):
            at_row = tail * (FULL + k * 64) + (1 - tail) * (9 * C + k * C + (j - c) * 64)
            h_s[pl.ds(pl.multiple_of(at_row, 64), 64)] = block[j * 64 : (j + 1) * 64, k * C : (k + 1) * C]
    h_s[pl.ds(FULL + 192, 64)] = jnp.zeros((64, C), BF16)

    start(7, ring_sends(4, x, "dx", chunk(XO, XP), lambda j: x1.at[j]), x1.at[pl.ds(0, 3)])
    y1[y] = chunk(YO, YP)(y)[...]
    z1[z] = chunk(ZO, ZP)(z)[...]
    x1[x] = chunk(XO, XP)(x)[...]
    for i in range(X):
        rows = pl.ds(pl.multiple_of((own + i) * PLANE, PLANE), PLANE)
        dpad[1 + i, 1 : 1 + Y] = dhc_s[rows, C : 2 * C].reshape(Y, Z, C)
    gg_out[...] = gain_grad
    sg_out[...] = shift_grad

    def add_up(buf, n):
        acc = buf[0].astype(F32)
        for j in range(1, n):
            acc = acc + buf[j].astype(F32)
        return acc

    wait_bytes(rsem.at[5], y1.at[pl.ds(0, 7)])
    s2y[...] = add_up(y1, 8).reshape(8, YP // 8, C)
    y2[z] = s2y[z]
    start(8, ring_sends(8, z, "dz", lambda j: s2y.at[j], lambda j: y2.at[j]), y2.at[pl.ds(0, 7)])
    wait_bytes(rsem.at[6], z1.at[pl.ds(0, 7)])
    s2z[...] = add_up(z1, 8).reshape(8, ZP // 8, C)
    z2[y] = s2z[y]
    start(9, ring_sends(8, y, "dy", lambda j: s2z.at[j], lambda j: z2.at[j]), z2.at[pl.ds(0, 7)])
    wait_bytes(rsem.at[7], x1.at[pl.ds(0, 3)])
    s2x[...] = add_up(x1, 4).reshape(8, XP // 8, C)
    x2[y] = s2x[y]
    start(10, ring_sends(8, y, "dy", lambda j: s2x.at[j], lambda j: x2.at[j]), x2.at[pl.ds(0, 7)])

    inner_x = pl.ds(1, X)
    moves = [
        (X, inner, 0, inner, (up_x, gy)),
        (1, inner, X + 1, inner, (down_x, gy)),
        (inner_x, Y, inner_x, 0, (gx, up_y)),
        (inner_x, 1, inner_x, Y + 1, (gx, down_y)),
        (X, Y, 0, 0, (up_x, up_y)),
        (X, 1, 0, Y + 1, (up_x, down_y)),
        (1, Y, X + 1, 0, (down_x, up_y)),
        (1, 1, X + 1, Y + 1, (down_x, down_y)),
    ]
    dh_bytes = gwbuf.at[pl.ds(0, (4 * (Y + 2) - COLS) * Z)]
    start(11, [(0, dpad.at[a, b], dpad.at[d, e], dev) for a, b, d, e, dev in moves], dh_bytes)

    wait_bytes(rsem.at[10], x2.at[pl.ds(0, 7)])
    x3[z] = add_up(x2, 8)
    start(12, ring_sends(8, z, "dz", lambda j: x3.at[z], lambda j: x3.at[j]), x3.at[pl.ds(0, 7)])
    wait_bytes(rsem.at[8], y2.at[pl.ds(0, 7)])
    y3[x] = add_up(y2, 8)
    start(13, ring_sends(4, x, "dx", lambda j: y3.at[x], lambda j: y3.at[j]), y3.at[pl.ds(0, 3)])
    wait_bytes(rsem.at[9], z2.at[pl.ds(0, 7)])
    z3[x] = add_up(z2, 8)
    start(14, ring_sends(4, x, "dx", lambda j: z3.at[x], lambda j: z3.at[j]), z3.at[pl.ds(0, 3)])

    wait_bytes(rsem.at[11], dh_bytes)
    clear(gx == 0, dpad.at[0])
    clear(gx == 31, dpad.at[X + 1])
    clear(gy == 0, dpad.at[:, 0])
    clear(gy == 15, dpad.at[:, Y + 1])
    for i in range(X):
        total = jnp.zeros((PLANE, 3 * C), F32)
        for ab in range(9):
            a, b = ab // 3, ab % 3
            moved = dpad[i + 2 - a, 2 - b : 2 - b + Y].reshape(PLANE, C)
            total = total + lax.dot_general(
                moved, w_v[pl.ds(ab * 3 * C, 3 * C)], NT, preferred_element_type=F32
            )
        minus = jnp.where(zrow == Z - 1, 0.0, pltpu.roll(total[:, 0:C], PLANE - 1, 0))
        plus = jnp.where(zrow == 0, 0.0, pltpu.roll(total[:, 2 * C : 3 * C], 1, 0))
        gin_out[i] = (total[:, C : 2 * C] + minus + plus).astype(BF16).reshape(Y, Z, C)

    wait_bytes(rsem.at[13], y3.at[pl.ds(0, 3)])
    y4[z] = add_up(y3, 4)
    start(15, ring_sends(8, z, "dz", lambda j: y4.at[z], lambda j: y4.at[j]), y4.at[pl.ds(0, 7)])
    wait_bytes(rsem.at[14], z3.at[pl.ds(0, 3)])
    z4[y] = add_up(z3, 4)
    start(16, ring_sends(8, y, "dy", lambda j: z4.at[y], lambda j: z4.at[j]), z4.at[pl.ds(0, 7)])
    wait_bytes(rsem.at[12], x3.at[pl.ds(0, 7)])
    x4[y] = add_up(x3, 8)
    start(17, ring_sends(8, y, "dy", lambda j: x4.at[y], lambda j: x4.at[j]), x4.at[pl.ds(0, 7)])

    half, half_other = c * HALF, (1 - c) * HALF
    spans = (
        (15, y4, 18, 21, 8, y, "dy", YO, YP), (16, z4, 19, 22, 8, z, "dz", ZO, ZP),
        (17, x4, 20, 23, 4, x, "dx", XO, XP),
    )

    def place(base, j, size):
        return gwbuf.at[pl.ds(pl.multiple_of(half + base + j * size, 64), size)]

    for stage, buf, out, onward, n, me, axis, base, size in spans:
        wait_bytes(rsem.at[stage], buf.at[pl.ds(0, 7)])
        ref = place(base, me, size)
        ref[...] = buf[...].reshape(size, C).astype(BF16)
        for k in ring(n):
            send(out, ref, ref, at(**{axis: k}))
        pending.append((out, gwbuf.at[pl.ds(0, (n - 1) * size)]))
    for stage, buf, out, onward, n, me, axis, base, size in spans[2:] + spans[:2]:
        wait_bytes(rsem.at[out], gwbuf.at[pl.ds(0, (n - 1) * size)])
        ref = gwbuf.at[pl.ds(pl.multiple_of(half + base, 64), n * size)]
        start(onward, [(0, ref, ref, other)], gwbuf.at[pl.ds(0, n * size)])

    def write_half(core, base):
        moves = [(t * C, core * 18 * C + t * C, C) for t in range(9)]
        moves += [(t * C, core * 6 * C + t * C, C) for t in range(9, 12)]
        moves += [(FULL + k * 64, FULL + k * C + core * 64, 64) for k in range(3)]
        for src, dst, n in moves:
            gw_out[pl.ds(pl.multiple_of(dst, 64), n)] = gwbuf[pl.ds(pl.multiple_of(base + src, 64), n)]

    write_half(c, half)
    for _, _, _, onward, n, _, _, _, size in spans:
        wait_bytes(rsem.at[onward], gwbuf.at[pl.ds(0, n * size)])
    write_half(1 - c, half_other)
    for stage, ref in pending:
        wait_bytes(ssem.at[stage], ref)


def copy_out(*refs):
    n = len(refs) // 2
    ins, outs, sem = refs[:n], refs[n : 2 * n], refs[-1]
    copies = [pltpu.make_async_copy(ins[i], outs[i], sem.at[i]) for i in range(n)]
    for cp in copies:
        cp.start()
    for cp in copies:
        cp.wait()


def on_device(feat_in, conv_out, activ, weight, gain, head, labels, grad_up):
    total_voxels = VOX * lax.axis_size("gx") * lax.axis_size("gy") * 1.0
    hbm = pl.BlockSpec(memory_space=pltpu.HBM)
    anywhere = pl.BlockSpec(memory_space=pl.ANY)
    vmem = pl.BlockSpec(memory_space=pltpu.VMEM)
    V = pltpu.VMEM
    shapes = (
        jax.ShapeDtypeStruct((X, Y, Z, C), BF16),
        jax.ShapeDtypeStruct((27 * C, C), BF16),
        jax.ShapeDtypeStruct((1, C), F32),
        jax.ShapeDtypeStruct((1, C), F32),
    )
    operands = (
        feat_in, conv_out, activ, weight, gain.reshape(1, C), head, labels.transpose(1, 0, 2), grad_up
    )
    operands = [pltpu.with_memory_space_constraint(t, pltpu.HBM) for t in operands]
    outs = pl.pallas_call(
        functools.partial(kernel, total_voxels),
        out_shape=shapes,
        in_specs=[hbm] * 8,
        out_specs=(vmem,) * 4,
        scratch_shapes=[
            V((1, C), F32),
            V((3, C), F32),
            V((Y, X, Z), jnp.int32),
            V((6, Y + 2, Z, C), BF16),
            V((X + 2, Y + 2, Z, C), BF16),
            V((4, Y, Z, C), BF16),
            V((4, PLANE, C), F32),
            V((X, Y, Z, C), BF16),
            V((X, Y, Z, C), BF16),
            V((27 * C, C), BF16),
            V((C, C), F32),
            V((4 * PLANE, 3 * C), BF16),
            V((9 * C, 4 * PLANE), BF16),
            V((HALF, C), BF16),
            V((16, STATS, C), F32), V((32, STATS, C), F32),
            V((8, YP, C), BF16), V((8, ZP, C), BF16), V((4, XP, C), BF16),
            V((8, YP // 8, C), F32), V((8, ZP // 8, C), F32), V((8, XP // 8, C), F32),
            V((4, YP // 8, C), F32), V((4, ZP // 8, C), F32), V((8, XP // 8, C), F32),
            V((8, YP // 8, C), F32), V((8, ZP // 8, C), F32), V((8, XP // 8, C), F32),
            V((8, YP // 8, C), F32), V((8, ZP // 8, C), F32), V((8, XP // 8, C), F32),
            V((2 * HALF, C), BF16),
            pltpu.SemaphoreType.DMA((9,)),
            pltpu.SemaphoreType.DMA((24,)),
            pltpu.SemaphoreType.DMA((24,)),
            pltpu.SemaphoreType.REGULAR,
        ],
        compiler_params=pltpu.CompilerParams(
            collective_id=0, has_side_effects=True, vmem_limit_bytes=40 * 2**20
        ),
        name="conv_block_backward",
    )(*operands)
    gin, gw, gg, sg = pl.pallas_call(
        copy_out,
        out_shape=shapes,
        in_specs=[anywhere] * 4,
        out_specs=(hbm,) * 4,
        scratch_shapes=[pltpu.SemaphoreType.DMA((4,))],
        compiler_params=pltpu.CompilerParams(vmem_limit_bytes=4 * 2**20),
        name="copy_outputs",
    )(*outs)
    return gin, gw, gg.reshape(C), sg.reshape(C)


def solution(mesh):
    return jax.shard_map(
        on_device,
        mesh=mesh,
        in_specs=(
            P("gx", "gy", None, None),
            P("gx", "gy", None, None),
            P("gx", "gy", None, None),
            P(),
            P(),
            P(),
            P("gx", "gy", None),
            P("gx", "gy", None, None),
        ),
        out_specs=(P("gx", "gy", None, None), P(), P(), P()),
        check_vma=False,
    )
```

```python
import functools

import jax
import jax.numpy as jnp
from jax import lax
from jax.experimental import pallas as pl
from jax.experimental.pallas import tpu as pltpu
from jax.sharding import PartitionSpec as P

MESH = pl.DeviceIdType.MESH
F32 = jnp.float32
BF16 = jnp.bfloat16
C = 128
X, Y, Z = 2, 12, 32
COLS = X * Y
VOX = COLS * Z
PLANE = Y * Z
HALF = 14 * C
YP, ZP, XP = 64, 64, 192
YO, ZO, XO = 0, 8 * YP, 8 * YP + 8 * ZP
FULL = 12 * C
NT = (((1,), (1,)), ((), ()))
STATS = 4


def hops(k, n):
    return min(k, n - k)


def ring(n):
    return sorted(range(1, n), key=lambda k: -hops(k, n))


def kernel(
    total_voxels,
    feat, conv, activ, weight, gain_in, head_in, labels_in, grad_up,
    gin_out, gw_out, gg_out, sg_out,
    gain, head, labels, fpad, dpad, conv_v, dn_v, act_v, gu_v, w_v, lab_s, dhc_s, ft_s, h_s,
    ra, rb,
    y1, z1, x1, y2, z2, x2, y3, z3, x3, y4, z4, x4, s2y, s2z, s2x, gwbuf,
    lsem, ssem, rsem, late,
):
    gx, gy = lax.axis_index("gx"), lax.axis_index("gy")
    z, xl, c = gx // 4, (gx // 2) % 2, gx % 2
    xh, y = gy // 8, gy % 8
    x = xh * 2 + xl

    def at(dx=0, dy=0, dz=0, dc=0):
        ax = (x + dx) % 4
        return (((z + dz) % 8) * 4 + (ax % 2) * 2 + (c + dc) % 2, (ax // 2) * 8 + (y + dy) % 8)

    other = at(dc=1)
    chip = gx // 2
    ahead, behind = (chip + 1) % 16, (chip + 15) % 16
    up_y, down_y = (gy + 1) % 16, (gy + 15) % 16
    up_x, down_x = (gx + 1) % 32, (gx + 31) % 32
    across = c * ahead + (1 - c) * behind

    yc = [(0, k, 0, e) for k in range(8) for e in range(2) if (k, e) != (0, 0)]
    xz = [(j, 0, k, 0) for j in range(4) for k in range(8) if (j, k) != (0, 0)]

    def far_first(offsets):
        return sorted(offsets, key=lambda o: -(hops(o[0], 4) + hops(o[1], 8) + hops(o[2], 8)))

    barrier = pltpu.get_barrier_semaphore()

    def signal(sem, dev):
        pl.semaphore_signal(sem, inc=1, device_id=dev, device_id_type=MESH)

    rank = z * 4 + x

    def rank_of(o):
        return ((z + o[2]) % 8) * 4 + (x + o[0]) % 4

    partners = [at(*o) for o in far_first(yc)]
    partners += [(i, j) for i in (behind * 2 + 1, ahead * 2) for j in (down_y, gy, up_y)]
    partners += [(chip * 2 + e, j) for j in (down_y, up_y) for e in range(2)]
    partners += [(i, j) for i in (down_x, up_x) for j in (down_y, gy, up_y)]
    for p in partners[:15]:
        signal(barrier, p)

    own = 2 * c
    small = [
        pltpu.make_async_copy(labels_in, labels, lsem.at[6]),
        pltpu.make_async_copy(head_in, head, lsem.at[7]),
        pltpu.make_async_copy(gain_in, gain, lsem.at[8]),
    ]
    loads = [
        pltpu.make_async_copy(activ, act_v, lsem.at[0]),
        pltpu.make_async_copy(grad_up, gu_v, lsem.at[1]),
        pltpu.make_async_copy(conv, conv_v.at[pl.ds(own, X)], lsem.at[2]),
        pltpu.make_async_copy(feat, fpad.at[pl.ds(1 + own, X), pl.ds(1, Y)], lsem.at[3]),
        pltpu.make_async_copy(weight, w_v, lsem.at[4]),
    ]
    for cp in small + loads:
        cp.start()

    for p in partners[15:]:
        signal(barrier, p)
    for o in far_first(xz):
        @pl.when(rank_of(o) > rank)
        def _():
            signal(barrier, at(*o))

    pending = []

    def send(stage, src, dst, dev):
        pltpu.make_async_remote_copy(
            src_ref=src, dst_ref=dst, send_sem=ssem.at[stage], recv_sem=rsem.at[stage],
            device_id=dev, device_id_type=MESH,
        ).start()

    def ring_sends(n, me, axis, src, dst):
        return [
            (hops(k, n), src((me + k) % n), dst(me), at(**{axis: k})) for k in ring(n)
        ]

    def start(stage, sends, count):
        for _, src, dst, dev in sends:
            send(stage, src, dst, dev)
        pending.append((stage, count))

    def wait_bytes(sem, ref):
        pltpu.make_async_copy(ref, ref, sem).wait()

    for cp in small:
        cp.wait()

    lab_s[...] = jnp.zeros_like(lab_s)
    for i in range(X):
        lab_s[pl.ds(16 * i, Y), pl.ds(0, Z)] = labels[:, i].astype(F32)
    lab_t = jnp.transpose(lab_s[...])[0:Z]

    row = lax.broadcasted_iota(jnp.int32, (C, C), 0)
    rep = jnp.zeros((C, C), F32)
    for k in range(3):
        rep = jnp.where(row % 3 == k, head[k : k + 1, :], rep)
    rep = jnp.where(row < 18, rep, 0.0)
    hi = rep.astype(BF16)
    left = rep - hi.astype(F32)
    mid = left.astype(BF16)
    low = (left - mid.astype(F32)).astype(BF16)
    part = row // 3
    back = jnp.where(
        (part == 0) | (part == 3) | (part == 5), hi.astype(F32),
        jnp.where((part == 1) | (part == 4), mid.astype(F32),
                  jnp.where(part == 2, low.astype(F32), 0.0)),
    ).astype(BF16)
    lane = lax.broadcasted_iota(jnp.int32, (1, C), 1)
    lane_class = (lane % 3).astype(F32)

    loads[0].wait()
    act = act_v[...].reshape(VOX, C)
    logits = (
        lax.dot_general(act, hi, NT, preferred_element_type=F32)
        + lax.dot_general(act, mid, NT, preferred_element_type=F32)
        + lax.dot_general(act, low, NT, preferred_element_type=F32)
    )
    label = jnp.concatenate(
        [
            jnp.broadcast_to(lab_t[:, 16 * i + j : 16 * i + j + 1], (Z, C))
            for i in range(X) for j in range(Y)
        ],
        axis=0,
    )
    dz = 0.5 * (jax.nn.sigmoid(logits) - (label == lane_class).astype(F32))
    dz_hi = dz.astype(BF16).astype(F32)
    dz_left = dz - dz_hi
    dz_mid = dz_left.astype(BF16).astype(F32)
    dz_low = dz_left - dz_mid
    spread = jnp.where(lane < 9, dz_hi, jnp.where(lane < 15, dz_mid, dz_low)).astype(BF16)
    loads[1].wait()
    ga = gu_v[...].reshape(VOX, C).astype(F32) + jnp.dot(
        spread, back, preferred_element_type=F32
    )
    dn = jnp.where(act.astype(F32) > 0, ga, 0.01 * ga)
    dn_v[pl.ds(own, X)] = dn.reshape(X, PLANE, C)
    loads[2].wait()
    h = conv_v[pl.ds(own, X)].reshape(VOX, C).astype(F32)
    stats = jnp.concatenate(
        [
            jnp.sum(jnp.sum(term.reshape(VOX // 8, 8, C), axis=0), axis=0, keepdims=True)
            for term in (h, h * h, dn, dn * h)
        ],
        axis=0,
    )

    slot_a = c * 8 + y
    ra[slot_a] = stats
    pl.semaphore_wait(barrier, len(partners) + rank)
    for o in far_first(xz):
        @pl.when(rank_of(o) < rank)
        def _():
            signal(late, at(*o))

    start(0, [(0, ra.at[slot_a], ra.at[slot_a], at(*o)) for o in far_first(yc)], ra.at[pl.ds(0, 15)])

    loads[3].wait()
    inner, edge = pl.ds(1, Y), 1 + own
    near = 1 + own + c
    far = 5 * (1 - c)
    planes = fpad.at[pl.ds(edge, X), inner]
    rim = [(0, planes, planes, other)]
    for e in range(2):
        rim.append((0, fpad.at[near, inner], fpad.at[far, inner], (across * 2 + e, gy)))
        for here, there, dev in ((Y, 0, up_y), (1, Y + 1, down_y)):
            rim.append(
                (0, fpad.at[pl.ds(edge, X), here], fpad.at[pl.ds(edge, X), there], (chip * 2 + e, dev))
            )
            rim.append((0, fpad.at[near, here], fpad.at[far, there], (across * 2 + e, dev)))
    rim_bytes = gwbuf.at[pl.ds(0, (6 * (Y + 2) - COLS) * Z)]
    start(1, rim, rim_bytes)
    mine = conv_v.at[pl.ds(own, X)]
    start(2, [(0, mine, mine, other)], conv_v.at[pl.ds(0, X)])
    mine = dn_v.at[pl.ds(own, X)]
    start(3, [(0, mine, mine, other)], dn_v.at[pl.ds(0, X)])

    wait_bytes(rsem.at[0], ra.at[pl.ds(0, 15)])
    slot_b = x * 8 + z
    rb[slot_b] = jnp.sum(ra[...], axis=0)

    @pl.when(rank < 31)
    def _():
        pl.semaphore_wait(late, 31 - rank)

    start(4, [(0, rb.at[slot_b], rb.at[slot_b], at(*o)) for o in far_first(xz)], rb.at[pl.ds(0, 31)])

    wait_bytes(rsem.at[1], rim_bytes)

    def clear(cond, ref):
        @pl.when(cond)
        def _():
            ref[...] = jnp.zeros(ref.shape, BF16)

    clear(chip == 0, fpad.at[0])
    clear(chip == 15, fpad.at[5])
    clear(gy == 0, fpad.at[:, 0])
    clear(gy == 15, fpad.at[:, Y + 1])
    for pln in range(6):
        for b in range(3):
            block = jnp.transpose(fpad[pln, b : b + Y].reshape(PLANE, C))
            for a in range(3):
                if 0 <= pln - a < 4:
                    ft_s[(3 * a + b) * C : (3 * a + b + 1) * C, (pln - a) * PLANE : (pln - a + 1) * PLANE] = block
    loads[4].wait()
    wait_bytes(rsem.at[2], conv_v.at[pl.ds(0, X)])
    wait_bytes(rsem.at[3], dn_v.at[pl.ds(0, X)])

    wait_bytes(rsem.at[4], rb.at[pl.ds(0, 31)])
    stats = jnp.sum(rb[...], axis=0)
    mean = stats[0:1] / total_voxels
    rstd = lax.rsqrt(stats[1:2] / total_voxels - mean * mean + 1e-05)
    shift_grad = stats[2:3]
    gain_grad = rstd * (stats[3:4] - mean * shift_grad)
    scale = gain[...] * rstd
    shift_mean = shift_grad / total_voxels
    gain_mean = gain_grad / total_voxels

    zrow = lax.broadcasted_iota(jnp.int32, (PLANE, C), 0) & (Z - 1)
    for p in range(4):
        hp = conv_v[p].reshape(PLANE, C).astype(F32)
        dh = scale * (dn_v[p] - shift_mean - (hp - mean) * rstd * gain_mean)
        rows = pl.ds(p * PLANE, PLANE)
        after = jnp.where(zrow == Z - 1, 0.0, pltpu.roll(dh, PLANE - 1, 0))
        before = jnp.where(zrow == 0, 0.0, pltpu.roll(dh, 1, 0))
        dhc_s[rows, 0:C] = after.astype(BF16)
        dhc_s[rows, C : 2 * C] = dh.astype(BF16)
        dhc_s[rows, 2 * C : 3 * C] = before.astype(BF16)

    def chunk(base, size):
        return lambda j: h_s.at[pl.ds(pl.multiple_of(base + j * size, 64), size)]

    block = jnp.dot(
        ft_s[pl.ds(pl.multiple_of(c * 6 * C, C), 3 * C)], dhc_s[...], preferred_element_type=F32
    ).astype(BF16)
    for f in range(3):
        for k in range(3):
            h_s[pl.ds((f * 3 + k) * C, C)] = block[f * C : (f + 1) * C, k * C : (k + 1) * C]
    first = ring_sends(8, y, "dy", chunk(YO, YP), lambda j: y1.at[j])
    second = ring_sends(8, z, "dz", chunk(ZO, ZP), lambda j: z1.at[j])
    for sy, sz in zip(first, second):
        send(5, *sy[1:])
        send(6, *sz[1:])
    pending.append((5, y1.at[pl.ds(0, 7)]))
    pending.append((6, z1.at[pl.ds(0, 7)]))
    block = jnp.dot(
        ft_s[pl.ds(pl.multiple_of(3 * C + c * 192, 64), 192)], dhc_s[...], preferred_element_type=F32
    ).astype(BF16)
    for j in range(3):
        tail = (1 - c) if j == 2 else (c if j == 0 else 0)
        for k in range(3):
            at_row = tail * (FULL + k * 64) + (1 - tail) * (9 * C + k * C + (j - c) * 64)
            h_s[pl.ds(pl.multiple_of(at_row, 64), 64)] = block[j * 64 : (j + 1) * 64, k * C : (k + 1) * C]
    h_s[pl.ds(FULL + 192, 64)] = jnp.zeros((64, C), BF16)

    start(7, ring_sends(4, x, "dx", chunk(XO, XP), lambda j: x1.at[j]), x1.at[pl.ds(0, 3)])
    y1[y] = chunk(YO, YP)(y)[...]
    z1[z] = chunk(ZO, ZP)(z)[...]
    x1[x] = chunk(XO, XP)(x)[...]
    for i in range(X):
        rows = pl.ds(pl.multiple_of((own + i) * PLANE, PLANE), PLANE)
        dpad[1 + i, 1 : 1 + Y] = dhc_s[rows, C : 2 * C].reshape(Y, Z, C)
    gg_out[...] = gain_grad
    sg_out[...] = shift_grad

    def add_up(buf, n):
        acc = buf[0].astype(F32)
        for j in range(1, n):
            acc = acc + buf[j].astype(F32)
        return acc

    wait_bytes(rsem.at[7], x1.at[pl.ds(0, 3)])
    s2x[...] = add_up(x1, 4).reshape(8, XP // 8, C)
    x2[y] = s2x[y]
    start(10, ring_sends(8, y, "dy", lambda j: s2x.at[j], lambda j: x2.at[j]), x2.at[pl.ds(0, 7)])

    wait_bytes(rsem.at[5], y1.at[pl.ds(0, 7)])
    s2y[...] = add_up(y1, 8).reshape(8, YP // 8, C)
    y2[z] = s2y[z]
    start(8, ring_sends(8, z, "dz", lambda j: s2y.at[j], lambda j: y2.at[j]), y2.at[pl.ds(0, 7)])
    wait_bytes(rsem.at[6], z1.at[pl.ds(0, 7)])
    s2z[...] = add_up(z1, 8).reshape(8, ZP // 8, C)
    z2[y] = s2z[y]
    start(9, ring_sends(8, y, "dy", lambda j: s2z.at[j], lambda j: z2.at[j]), z2.at[pl.ds(0, 7)])
    inner_x = pl.ds(1, X)
    moves = [
        (X, inner, 0, inner, (up_x, gy)),
        (1, inner, X + 1, inner, (down_x, gy)),
        (inner_x, Y, inner_x, 0, (gx, up_y)),
        (inner_x, 1, inner_x, Y + 1, (gx, down_y)),
        (X, Y, 0, 0, (up_x, up_y)),
        (X, 1, 0, Y + 1, (up_x, down_y)),
        (1, Y, X + 1, 0, (down_x, up_y)),
        (1, 1, X + 1, Y + 1, (down_x, down_y)),
    ]
    dh_bytes = gwbuf.at[pl.ds(0, (4 * (Y + 2) - COLS) * Z)]
    start(11, [(0, dpad.at[a, b], dpad.at[d, e], dev) for a, b, d, e, dev in moves], dh_bytes)

    wait_bytes(rsem.at[10], x2.at[pl.ds(0, 7)])
    x3[z] = add_up(x2, 8)
    start(12, ring_sends(8, z, "dz", lambda j: x3.at[z], lambda j: x3.at[j]), x3.at[pl.ds(0, 7)])
    wait_bytes(rsem.at[8], y2.at[pl.ds(0, 7)])
    y3[x] = add_up(y2, 8)
    start(13, ring_sends(4, x, "dx", lambda j: y3.at[x], lambda j: y3.at[j]), y3.at[pl.ds(0, 3)])
    wait_bytes(rsem.at[9], z2.at[pl.ds(0, 7)])
    z3[x] = add_up(z2, 8)
    start(14, ring_sends(4, x, "dx", lambda j: z3.at[x], lambda j: z3.at[j]), z3.at[pl.ds(0, 3)])

    wait_bytes(rsem.at[11], dh_bytes)
    clear(gx == 0, dpad.at[0])
    clear(gx == 31, dpad.at[X + 1])
    clear(gy == 0, dpad.at[:, 0])
    clear(gy == 15, dpad.at[:, Y + 1])
    for i in range(X):
        total = jnp.zeros((PLANE, 3 * C), F32)
        for ab in range(9):
            a, b = ab // 3, ab % 3
            moved = dpad[i + 2 - a, 2 - b : 2 - b + Y].reshape(PLANE, C)
            total = total + lax.dot_general(
                moved, w_v[pl.ds(ab * 3 * C, 3 * C)], NT, preferred_element_type=F32
            )
        minus = jnp.where(zrow == Z - 1, 0.0, pltpu.roll(total[:, 0:C], PLANE - 1, 0))
        plus = jnp.where(zrow == 0, 0.0, pltpu.roll(total[:, 2 * C : 3 * C], 1, 0))
        gin_out[i] = (total[:, C : 2 * C] + minus + plus).astype(BF16).reshape(Y, Z, C)

    wait_bytes(rsem.at[13], y3.at[pl.ds(0, 3)])
    y4[z] = add_up(y3, 4)
    start(15, ring_sends(8, z, "dz", lambda j: y4.at[z], lambda j: y4.at[j]), y4.at[pl.ds(0, 7)])
    wait_bytes(rsem.at[14], z3.at[pl.ds(0, 3)])
    z4[y] = add_up(z3, 4)
    start(16, ring_sends(8, y, "dy", lambda j: z4.at[y], lambda j: z4.at[j]), z4.at[pl.ds(0, 7)])
    wait_bytes(rsem.at[12], x3.at[pl.ds(0, 7)])
    x4[y] = add_up(x3, 8)
    start(17, ring_sends(8, y, "dy", lambda j: x4.at[y], lambda j: x4.at[j]), x4.at[pl.ds(0, 7)])

    half, half_other = c * HALF, (1 - c) * HALF
    spans = (
        (15, y4, 18, 21, 8, y, "dy", YO, YP), (16, z4, 19, 22, 8, z, "dz", ZO, ZP),
        (17, x4, 20, 23, 4, x, "dx", XO, XP),
    )

    def place(base, j, size):
        return gwbuf.at[pl.ds(pl.multiple_of(half + base + j * size, 64), size)]

    for stage, buf, out, onward, n, me, axis, base, size in spans:
        wait_bytes(rsem.at[stage], buf.at[pl.ds(0, 7)])
        ref = place(base, me, size)
        ref[...] = buf[...].reshape(size, C).astype(BF16)
        for k in ring(n):
            send(out, ref, ref, at(**{axis: k}))
        pending.append((out, gwbuf.at[pl.ds(0, (n - 1) * size)]))
    for stage, buf, out, onward, n, me, axis, base, size in spans[2:] + spans[:2]:
        wait_bytes(rsem.at[out], gwbuf.at[pl.ds(0, (n - 1) * size)])
        ref = gwbuf.at[pl.ds(pl.multiple_of(half + base, 64), n * size)]
        start(onward, [(0, ref, ref, other)], gwbuf.at[pl.ds(0, n * size)])

    def write_half(core, base):
        moves = [(t * C, core * 18 * C + t * C, C) for t in range(9)]
        moves += [(t * C, core * 6 * C + t * C, C) for t in range(9, 12)]
        moves += [(FULL + k * 64, FULL + k * C + core * 64, 64) for k in range(3)]
        for src, dst, n in moves:
            gw_out[pl.ds(pl.multiple_of(dst, 64), n)] = gwbuf[pl.ds(pl.multiple_of(base + src, 64), n)]

    write_half(c, half)
    for _, _, _, onward, n, _, _, _, size in spans:
        wait_bytes(rsem.at[onward], gwbuf.at[pl.ds(0, n * size)])
    write_half(1 - c, half_other)
    for stage, ref in pending:
        wait_bytes(ssem.at[stage], ref)


def copy_out(*refs):
    n = len(refs) // 2
    ins, outs, sem = refs[:n], refs[n : 2 * n], refs[-1]
    copies = [pltpu.make_async_copy(ins[i], outs[i], sem.at[i]) for i in range(n)]
    for cp in copies:
        cp.start()
    for cp in copies:
        cp.wait()


def on_device(feat_in, conv_out, activ, weight, gain, head, labels, grad_up):
    total_voxels = VOX * lax.axis_size("gx") * lax.axis_size("gy") * 1.0
    hbm = pl.BlockSpec(memory_space=pltpu.HBM)
    anywhere = pl.BlockSpec(memory_space=pl.ANY)
    vmem = pl.BlockSpec(memory_space=pltpu.VMEM)
    V = pltpu.VMEM
    shapes = (
        jax.ShapeDtypeStruct((X, Y, Z, C), BF16),
        jax.ShapeDtypeStruct((27 * C, C), BF16),
        jax.ShapeDtypeStruct((1, C), F32),
        jax.ShapeDtypeStruct((1, C), F32),
    )
    operands = (
        feat_in, conv_out, activ, weight, gain.reshape(1, C), head, labels.transpose(1, 0, 2), grad_up
    )
    operands = [pltpu.with_memory_space_constraint(t, pltpu.HBM) for t in operands]
    outs = pl.pallas_call(
        functools.partial(kernel, total_voxels),
        out_shape=shapes,
        in_specs=[hbm] * 8,
        out_specs=(vmem,) * 4,
        scratch_shapes=[
            V((1, C), F32),
            V((3, C), F32),
            V((Y, X, Z), jnp.int32),
            V((6, Y + 2, Z, C), BF16),
            V((X + 2, Y + 2, Z, C), BF16),
            V((4, Y, Z, C), BF16),
            V((4, PLANE, C), F32),
            V((X, Y, Z, C), BF16),
            V((X, Y, Z, C), BF16),
            V((27 * C, C), BF16),
            V((C, C), F32),
            V((4 * PLANE, 3 * C), BF16),
            V((9 * C, 4 * PLANE), BF16),
            V((HALF, C), BF16),
            V((16, STATS, C), F32), V((32, STATS, C), F32),
            V((8, YP, C), BF16), V((8, ZP, C), BF16), V((4, XP, C), BF16),
            V((8, YP // 8, C), F32), V((8, ZP // 8, C), F32), V((8, XP // 8, C), F32),
            V((4, YP // 8, C), F32), V((4, ZP // 8, C), F32), V((8, XP // 8, C), F32),
            V((8, YP // 8, C), F32), V((8, ZP // 8, C), F32), V((8, XP // 8, C), F32),
            V((8, YP // 8, C), F32), V((8, ZP // 8, C), F32), V((8, XP // 8, C), F32),
            V((2 * HALF, C), BF16),
            pltpu.SemaphoreType.DMA((9,)),
            pltpu.SemaphoreType.DMA((24,)),
            pltpu.SemaphoreType.DMA((24,)),
            pltpu.SemaphoreType.REGULAR,
        ],
        compiler_params=pltpu.CompilerParams(
            collective_id=0, has_side_effects=True, vmem_limit_bytes=40 * 2**20
        ),
        name="conv_block_backward",
    )(*operands)
    gin, gw, gg, sg = pl.pallas_call(
        copy_out,
        out_shape=shapes,
        in_specs=[anywhere] * 4,
        out_specs=(hbm,) * 4,
        scratch_shapes=[pltpu.SemaphoreType.DMA((4,))],
        compiler_params=pltpu.CompilerParams(vmem_limit_bytes=4 * 2**20),
        name="copy_outputs",
    )(*outs)
    return gin, gw, gg.reshape(C), sg.reshape(C)


def solution(mesh):
    return jax.shard_map(
        on_device,
        mesh=mesh,
        in_specs=(
            P("gx", "gy", None, None),
            P("gx", "gy", None, None),
            P("gx", "gy", None, None),
            P(),
            P(),
            P(),
            P("gx", "gy", None),
            P("gx", "gy", None, None),
        ),
        out_specs=(P("gx", "gy", None, None), P(), P(), P()),
        check_vma=False,
    )
```
